512 devices in a mesh: dp: 16 (over x, y), cent: 32 (over z, core).
Axes of the slice: x: 4, y: 4, z: 16, core: 2. Of those that a mesh axis runs over, the one named last changes fastest.
Arguments:
- embeddings: bfloat16 [32768, 768], P(('dp', 'cent')), may hold values from -60 to 60, as said below
- candidates: int32 [32768, 32], P('dp'), may hold values from 0 to 255, all different within a row
- centroids: bfloat16 [32768, 768], P('cent'), may hold values from -5 to 7, as said below
Outputs:
- new_centroids: float32 [32768, 768], P('cent', 'dp')
The draws below stay inside these ranges and needn't reach their ends.
Inputs may be any that keep to these rules, and one draw needn't show every extreme that they name: Real-valued embeddings. Real-valued centroids. `candidates`: each row lists 32 different blocks; every block is listed by some row.
All inputs are finite; a program needn't handle non-finite values.
Results may differ from the reference program's by a relative error of at most 0.0003.
Values may be sent and summed in bfloat16 or wider, within the bound.
A program may use at most 64 MiB of HBM per device.

```python
import math
import jax
import jax.numpy as jnp
from jax import lax

D = 768
BLOCK = 128
NCAND = 32
NB = 256
K = 32768
NVEC = 32768


def draw_centroids(key, part):
    key = jax.random.fold_in(key, 3)
    base = jnp.clip(jax.random.normal(key, (K, D), jnp.float32), -6.0, 6.0) + 1.0
    return base.astype(jnp.bfloat16)


def draw_embeddings(key, part):
    key = jax.random.fold_in(key, 5)
    first = jax.random.fold_in(key, 0)
    fourth = jax.random.fold_in(key, 2)
    values = jnp.clip(jax.random.normal(first, (NVEC, D), jnp.float32), -6.0, 6.0)
    strength = 1.0 + (110.0 + 150.0 * jax.random.uniform(fourth, (NVEC, 1), jnp.float32)) / math.sqrt(D)
    aligned = strength * jnp.ones((NVEC, D), jnp.float32)
    rows_idx = jnp.arange(NVEC, dtype=jnp.int32)
    chosen = (rows_idx % 61 == 0)[:, None]
    values = jnp.where(chosen, aligned, values)
    values = jnp.clip(values, -60.0, 60.0)
    return values.astype(jnp.bfloat16)


def different_ones(rng, rows, number_of, top, lift):
    order = jax.random.permutation(jax.random.fold_in(rng, 1), number_of)
    pull = order
    for power in range(3):
        pull = pull * pull // number_of
    pull = pull * lift // number_of
    tickets = jax.random.randint(jax.random.fold_in(rng, 2), (rows, number_of), 0, 4096) + pull
    fixed_rows = jax.random.permutation(jax.random.fold_in(rng, 3), rows)[jnp.arange(number_of) % rows]
    tickets = jnp.where(jnp.arange(rows)[:, None] == fixed_rows[None, :], 1 << 14, tickets)
    priority = tickets * number_of + jnp.arange(number_of)
    return lax.top_k(priority.astype(jnp.int32), top)[1].astype(jnp.int32)


def setup_inputs(seed: int = 0) -> dict:
    key_of = jax.random.split(jax.random.key(seed), 4)
    embeddings = draw_embeddings(jax.random.fold_in(key_of[3], 71), 0)
    candidates = different_ones(key_of[1], NVEC, NB, NCAND, 2048)
    centroids = draw_centroids(jax.random.fold_in(key_of[3], 71), 0)
    return dict(embeddings=embeddings, candidates=candidates, centroids=centroids)


def reference(embeddings, candidates, centroids):
    score_scale = 1.0 / math.sqrt(D)
    cent_f32 = centroids.astype(jnp.float32)
    half_sq = 0.5 * lax.optimization_barrier(jnp.sum(cent_f32 * cent_f32, axis=1))
    blocks = centroids.reshape(NB, BLOCK, D)
    half_blocks = half_sq.reshape(NB, BLOCK)
    row_block = math.gcd(NVEC, 128)
    vec_blocks = embeddings.reshape(NVEC // row_block, row_block, D)
    cand_blocks = candidates.reshape(NVEC // row_block, row_block, NCAND)

    def fold_block(state, inputs):
        sum_table, mass_table = state
        vectors, cand_rows = inputs
        vec_f32 = vectors.astype(jnp.float32)

        def one_logit(index):
            chosen = blocks[cand_rows[:, index]].astype(jnp.float32)
            dots = jnp.einsum('nd,nkd->nk', vec_f32, chosen)
            return (dots - half_blocks[cand_rows[:, index]]) * score_scale
        logits = lax.map(one_logit, jnp.arange(NCAND, dtype=jnp.int32))
        row_max = lax.optimization_barrier(jnp.max(logits, axis=(0, 2)))
        exps = jnp.exp(logits - row_max[None, :, None])
        row_total = lax.optimization_barrier(jnp.sum(exps, axis=(0, 2)))
        weights = exps / row_total[None, :, None]
        weights_bf = weights.astype(jnp.bfloat16).astype(jnp.float32)

        def add_one(tables, index):
            sums_now, mass_now = tables
            ids = cand_rows[:, index]
            contrib = jnp.einsum('nk,nd->nkd', weights_bf[index], vec_f32)
            sums_now = sums_now.at[ids].add(contrib)
            mass_now = mass_now.at[ids].add(weights[index])
            return ((sums_now, mass_now), None)
        (sum_table, mass_table), _ = lax.scan(add_one, (sum_table, mass_table), jnp.arange(NCAND, dtype=jnp.int32))
        return ((sum_table, mass_table), None)
    start = (jnp.zeros((NB, BLOCK, D), jnp.float32), jnp.zeros((NB, BLOCK), jnp.float32))
    (sum_table, mass_table), _ = lax.scan(fold_block, start, (vec_blocks, cand_blocks))
    sums = sum_table.reshape(K, D)
    mass = mass_table.reshape(K)
    return (sums + cent_f32) / (mass[:, None] + 1.0)
```

```python
import math

import jax
import jax.numpy as jnp
from jax import lax
from jax.experimental import pallas as pl
from jax.experimental.pallas import tpu as pltpu
from jax.sharding import PartitionSpec as P

D = 768
BLOCK = 128
Z = 16
SIDE = 4
SHARD = 64
CHUNK = 128
ROWS = Z * CHUNK
OWN = 1024
NBLK = OWN // BLOCK
COLS = 48
QN = 4
QW = OWN // QN
NCAND = 32
LOW = -1e30
FLOOR = -1e29
MESH = pl.DeviceIdType.MESH
NT = (((1,), (1,)), ((), ()))


def rem(a, b):
    return lax.rem(a, b)


def kernel(emb_hbm, cand_hbm, cent_hbm, out_ref,
           e_all, et, cent, cand, candt, hs, x_buf, w_buf, st, sb, fr, fac,
           mp, mass, mx, my, s_buf, rel1, dir1, rrl1, tmp1, r1, rel2, dir2, rrl2, tmp2, res,
           in_sem, ag_send, ag_recv, sib_send, sib_recv, st_send, st_recv, fr_send, fr_recv,
           m_send, m_recv, rs_send, rs_recv):
    dp = lax.axis_index("dp")
    ce = lax.axis_index("cent")
    z = ce // 2
    core = rem(ce, 2)
    px = dp // SIDE
    py = rem(dp, SIDE)
    right = rem(z + 1, Z)
    left = rem(z + Z - 1, Z)
    own = pl.ds(pl.multiple_of(core * SHARD, SHARD), SHARD)

    def dev(d, c):
        return (d, c)

    load_e = pltpu.make_async_copy(emb_hbm, e_all.at[0, own], in_sem.at[0])
    load_c = pltpu.make_async_copy(cent_hbm, cent, in_sem.at[1])
    load_k = pltpu.make_async_copy(cand_hbm, cand, in_sem.at[2])
    load_e.start()
    load_c.start()
    load_k.start()

    barrier = pltpu.get_barrier_semaphore()

    def greet_z(i, carry):
        pl.semaphore_signal(barrier, inc=1, device_id=dev(dp, rem(ce + i, 2 * Z)), device_id_type=MESH)
        return carry

    def greet_xy(k, carry):
        pl.semaphore_signal(barrier, inc=1, device_id=dev(rem(px + k, SIDE) * SIDE + py, ce), device_id_type=MESH)
        pl.semaphore_signal(barrier, inc=1, device_id=dev(px * SIDE + rem(py + k, SIDE), ce), device_id_type=MESH)
        return carry

    lax.fori_loop(1, 2 * Z, greet_z, 0)
    lax.fori_loop(1, SIDE, greet_xy, 0)
    pl.semaphore_wait(barrier, 2 * Z - 1 + 2 * (SIDE - 1))

    def hop(src, dst, rows, to_z):
        return pltpu.make_async_remote_copy(
            src_ref=e_all.at[src, rows], dst_ref=e_all.at[dst, rows],
            send_sem=ag_send.at[dst], recv_sem=ag_recv.at[dst],
            device_id=dev(dp, to_z * 2 + core), device_id_type=MESH)

    half_a = pl.ds(pl.multiple_of(core * SHARD, SHARD // 2), SHARD // 2)
    half_b = pl.ds(pl.multiple_of(core * SHARD + SHARD // 2, SHARD // 2), SHARD // 2)

    def hop_half(src, rows, sem, to_z):
        return pltpu.make_async_remote_copy(
            src_ref=e_all.at[src, rows], dst_ref=e_all.at[Z - 1, rows],
            send_sem=ag_send.at[sem], recv_sem=ag_recv.at[sem],
            device_id=dev(dp, to_z * 2 + core), device_id_type=MESH)

    def to_sibling(slot, rows):
        return pltpu.make_async_remote_copy(
            src_ref=e_all.at[slot, rows], dst_ref=e_all.at[slot, rows],
            send_sem=sib_send.at[slot], recv_sem=sib_recv.at[slot],
            device_id=dev(dp, z * 2 + 1 - core), device_id_type=MESH)

    other = pl.ds(pl.multiple_of((1 - core) * SHARD, SHARD), SHARD)

    load_e.wait()
    hop(0, 1, own, right).start()
    hop(0, 2, own, left).start()
    to_sibling(0, own).start()

    load_k.wait()
    for k in range(Z):
        part = cand[k * CHUNK:(k + 1) * CHUNK, :]
        wide = jnp.concatenate([part, jnp.zeros((CHUNK, BLOCK - NCAND), jnp.int32)], axis=1)
        candt[:, k * CHUNK:(k + 1) * CHUNK] = jnp.transpose(wide)[0:NCAND, :]
    load_c.wait()

    def square(b, carry):
        at = pl.ds(pl.multiple_of(b * BLOCK, BLOCK), BLOCK)
        c32 = cent[at, :].astype(jnp.float32)
        half = 0.5 * jnp.sum(c32 * c32, axis=1, keepdims=True)
        hs[at, :] = jnp.broadcast_to(half, (BLOCK, CHUNK))
        return carry

    lax.fori_loop(0, NBLK, square, 0)

    def source(i):
        odd = rem(i, 2)
        return rem(z + (1 - 2 * odd) * ((i + 1) // 2) + Z, Z)

    def holder(i):
        odd = rem(i, 2)
        return rem(z - (1 - 2 * odd) * ((i + 1) // 2) + Z, Z)

    def give_stats(i, c):
        return pltpu.make_async_remote_copy(
            src_ref=st.at[i], dst_ref=sb.at[2 * i + core],
            send_sem=st_send.at[2 * i + c], recv_sem=st_recv.at[2 * i + core],
            device_id=dev(dp, source(i) * 2 + c), device_id_type=MESH)

    scale = 1.0 / math.sqrt(D)

    def chunk(i, carry):
        to_sibling(i, other).wait_recv()
        lanes = pl.ds(pl.multiple_of(i * CHUNK, CHUNK), CHUNK)
        e = e_all[i]
        et[:, lanes] = jnp.transpose(e)
        listed = candt[:, pl.ds(pl.multiple_of(source(i) * CHUNK, CHUNK), CHUNK)]
        top = jnp.full((8, CHUNK), FLOOR, jnp.float32)
        for b in range(NBLK):
            dots = lax.dot_general(cent[b * BLOCK:(b + 1) * BLOCK, :], e, NT, preferred_element_type=jnp.float32)
            hit = jnp.max(jnp.where(listed == ce * NBLK + b, 1.0, 0.0), axis=0, keepdims=True)
            l = (dots - hs[b * BLOCK:(b + 1) * BLOCK, :]) * scale
            l = jnp.where(hit > 0.5, l, LOW)
            x_buf[b * BLOCK:(b + 1) * BLOCK, lanes] = l
            top = jnp.maximum(top, jnp.max(l.reshape(BLOCK // 8, 8, CHUNK), axis=0))
        m = jnp.max(top, axis=0, keepdims=True)
        total = jnp.zeros((8, CHUNK), jnp.float32)
        for b in range(NBLK):
            ex = jnp.exp(x_buf[b * BLOCK:(b + 1) * BLOCK, lanes] - m)
            x_buf[b * BLOCK:(b + 1) * BLOCK, lanes] = ex
            total = total + jnp.sum(ex.reshape(BLOCK // 8, 8, CHUNK), axis=0)
        st[i, 0:1] = m
        st[i, 1:2] = jnp.sum(total, axis=0, keepdims=True)

        @pl.when(i == 0)
        def _():
            sb[core] = st[0]
            give_stats(i, 1 - core).start()

        @pl.when(i > 0)
        def _():
            give_stats(i, 0).start()
            give_stats(i, 1).start()

        return carry

    def step(s, carry):
        @pl.when(s <= 7)
        def _():
            hop(2 * s - 1, 2 * s - 1, own, right).wait_recv()

            @pl.when(s <= 6)
            def _():
                hop(2 * s - 1, 2 * s + 1, own, right).start()

            @pl.when(s == 7)
            def _():
                hop_half(13, half_a, 15, right).start()

            to_sibling(2 * s - 1, own).start()
            hop(2 * s, 2 * s, own, left).wait_recv()

            @pl.when(s <= 6)
            def _():
                hop(2 * s, 2 * s + 2, own, left).start()

            @pl.when(s == 7)
            def _():
                hop_half(14, half_b, 16, left).start()

            to_sibling(2 * s, own).start()

        @pl.when(s == 8)
        def _():
            hop_half(15, half_a, 15, right).wait_recv()
            hop_half(15, half_b, 16, left).wait_recv()
            to_sibling(15, own).start()

        lax.fori_loop(jnp.maximum(2 * s - 3, 0), jnp.minimum(2 * s - 1, Z), chunk, 0)
        return carry

    lax.fori_loop(1, 10, step, 0)

    def take_stats(k, carry):
        @pl.when(k != core)
        def _():
            pltpu.make_async_remote_copy(
                src_ref=st.at[0], dst_ref=sb.at[k], send_sem=st_send.at[k], recv_sem=st_recv.at[k],
                device_id=dev(dp, z * 2 + 1 - core), device_id_type=MESH).wait_recv()
        return carry

    lax.fori_loop(0, 2 * Z, take_stats, 0)
    big = jnp.full((1, CHUNK), FLOOR, jnp.float32)
    for k in range(2 * Z):
        big = jnp.maximum(big, sb[k, 0:1])
    tot = jnp.zeros((1, CHUNK), jnp.float32)
    for k in range(2 * Z):
        tot = tot + sb[k, 1:2] * jnp.exp(sb[k, 0:1] - big)
    fr[0, 0:1] = big
    fr[0, 1:2] = 1.0 / tot

    def hand_out(i):
        return pltpu.make_async_remote_copy(
            src_ref=fr.at[0], dst_ref=fr.at[i], send_sem=fr_send.at[i], recv_sem=fr_recv.at[i],
            device_id=dev(dp, holder(i) * 2 + core), device_id_type=MESH)

    def send_out(k, carry):
        hand_out(Z - k).start()
        return carry

    lax.fori_loop(1, Z, send_out, 0)

    def factor(i, carry):
        @pl.when(i > 0)
        def _():
            hand_out(i).wait_recv()
        lanes = pl.ds(pl.multiple_of(i * CHUNK, CHUNK), CHUNK)
        fac[0:1, lanes] = jnp.exp(st[i, 0:1] - fr[i, 0:1]) * fr[i, 1:2]
        return carry

    lax.fori_loop(0, Z, factor, 0)

    def neighbour(q, stage, way):
        along_x = rem(q + stage + 1, 2)
        along_y = 1 - along_x
        nx = rem(px + way * along_x + SIDE, SIDE)
        ny = rem(py + way * along_y + SIDE, SIDE)
        return dev(nx * SIDE + ny, ce)

    def place(q, stage):
        along_x = rem(q + stage + 1, 2)
        return px * along_x + py * (1 - along_x)

    def rs(src, dst, q, stage, part, way):
        k = ((q * 2 + stage) * 3 + part) * 2 + way
        return pltpu.make_async_remote_copy(
            src_ref=src, dst_ref=dst, send_sem=rs_send.at[k], recv_sem=rs_recv.at[k],
            device_id=neighbour(q, stage, 1 - 2 * way), device_id_type=MESH)

    lo2, hi2 = pl.ds(0, 2), pl.ds(2, 2)
    loc, hic = pl.ds(0, COLS // 2), pl.ds(COLS // 2, COLS // 2)

    def shift(a, k):
        return rem(a + k, SIDE)

    def first(q):
        a = place(q, 0)
        return [
            rs(s_buf.at[q, shift(a, 2), lo2], rel1.at[q, 0], q, 0, 0, 0),
            rs(s_buf.at[q, shift(a, 2), hi2], rel1.at[q, 1], q, 0, 0, 1),
            rs(s_buf.at[q, shift(a, 1), hi2], dir1.at[q, 0], q, 0, 1, 0),
            rs(s_buf.at[q, shift(a, 3), lo2], dir1.at[q, 1], q, 0, 1, 1),
        ]

    def second(q):
        return [
            rs(tmp1.at[q, 0], rrl1.at[q, 0], q, 0, 2, 0),
            rs(tmp1.at[q, 1], rrl1.at[q, 1], q, 0, 2, 1),
        ]

    def third(q):
        b = place(q, 1)
        return [
            rs(r1.at[q, shift(b, 2), loc], rel2.at[q, 0], q, 1, 0, 0),
            rs(r1.at[q, shift(b, 2), hic], rel2.at[q, 1], q, 1, 0, 1),
            rs(r1.at[q, shift(b, 1), hic], dir2.at[q, 0], q, 1, 1, 0),
            rs(r1.at[q, shift(b, 3), loc], dir2.at[q, 1], q, 1, 1, 1),
        ]

    def fourth(q):
        return [
            rs(tmp2.at[q, 0], rrl2.at[q, 0], q, 1, 2, 0),
            rs(tmp2.at[q, 1], rrl2.at[q, 1], q, 1, 2, 1),
        ]

    SUB = 32

    def add_up(q, carry):
        def weigh(r, c):
            at = pl.ds(pl.multiple_of(q * QW + r * SUB, SUB), SUB)
            w = x_buf[at, :] * fac[0:1, :]
            w_buf[pl.ds(pl.multiple_of(r * SUB, SUB), SUB), :] = w.astype(jnp.bfloat16)
            part = w[:, 0:128]
            for k in range(1, ROWS // 128):
                part = part + w[:, k * 128:(k + 1) * 128]
            mp[at, :] = part
            return c

        lax.fori_loop(0, QW // SUB, weigh, 0)
        swap = rem(q, 2)

        def tall(g, c):
            rows = pl.ds(pl.multiple_of(g * 384, 128), 384)
            y = lax.dot_general(et[rows, :], w_buf[...], NT, preferred_element_type=jnp.float32)
            for j in range(8):
                jx = g * 2 + j // 4
                jy = j % 4
                i0 = jx + swap * (jy - jx)
                i1 = jy + swap * (jx - jy)
                s_buf[q, i0, i1] = y[j * COLS:(j + 1) * COLS, :]
            return c

        lax.fori_loop(0, 2, tall, 0)
        for copy in first(q):
            copy.start()
        return carry

    lax.fori_loop(0, QN, add_up, 0)

    def mass_copy(src, dst, stage, k):
        along_x = 1 - stage
        nx = rem(px + k * along_x, SIDE)
        ny = rem(py + k * stage, SIDE)
        return pltpu.make_async_remote_copy(
            src_ref=src, dst_ref=dst.at[k], send_sem=m_send.at[stage * SIDE + k], recv_sem=m_recv.at[stage * SIDE + k],
            device_id=dev(nx * SIDE + ny, ce), device_id_type=MESH)

    for k in range(NBLK):
        turned = jnp.transpose(mp[k * 128:(k + 1) * 128, :])
        mx[0, 0:1, k * 128:(k + 1) * 128] = jnp.sum(turned, axis=0, keepdims=True)
    for k in range(1, SIDE):
        mass_copy(mx.at[0], mx, 0, k).start()

    def relay1(q, carry):
        a = place(q, 0)
        for copy in first(q)[0:2]:
            copy.wait_recv()
        tmp1[q, 0] = rel1[q, 0] + s_buf[q, shift(a, 1), lo2]
        tmp1[q, 1] = rel1[q, 1] + s_buf[q, shift(a, 3), hi2]
        for copy in second(q):
            copy.start()
        return carry

    lax.fori_loop(0, QN, relay1, 0)

    pick_r = lax.broadcasted_iota(jnp.int32, (COLS, D), 0)
    pick_c = lax.broadcasted_iota(jnp.int32, (COLS, D), 1)
    pick = jnp.where(pick_c == pick_r + dp * COLS, 1.0, 0.0).astype(jnp.bfloat16)
    for b in range(NBLK // 2):
        at = slice(b * QW, (b + 1) * QW)
        res[b] = lax.dot_general(pick, cent[at, :], NT, preferred_element_type=jnp.float32)

    for k in range(1, SIDE):
        mass_copy(mx.at[0], mx, 0, k).wait_recv()
    my[0] = (mx[0] + mx[1]) + (mx[2] + mx[3])
    for k in range(1, SIDE):
        mass_copy(my.at[0], my, 1, k).start()

    def close1(q, carry):
        a = place(q, 0)
        for copy in first(q)[2:4] + second(q):
            copy.wait_recv()
        r1[q, 0:2] = s_buf[q, a, lo2] + dir1[q, 1] + rrl1[q, 0]
        r1[q, 2:4] = s_buf[q, a, hi2] + dir1[q, 0] + rrl1[q, 1]
        for copy in third(q):
            copy.start()
        return carry

    lax.fori_loop(0, QN, close1, 0)

    def relay2(q, carry):
        b = place(q, 1)
        for copy in third(q)[0:2]:
            copy.wait_recv()
        tmp2[q, 0] = rel2[q, 0] + r1[q, shift(b, 1), loc]
        tmp2[q, 1] = rel2[q, 1] + r1[q, shift(b, 3), hic]
        for copy in fourth(q):
            copy.start()
        return carry

    lax.fori_loop(0, QN, relay2, 0)

    for k in range(1, SIDE):
        mass_copy(my.at[0], my, 1, k).wait_recv()
    mass[...] = 1.0 / ((my[0] + my[1]) + (my[2] + my[3]) + 1.0)

    def close2(q, carry):
        b = place(q, 1)
        for copy in third(q)[2:4] + fourth(q):
            copy.wait_recv()
        lanes = pl.ds(pl.multiple_of(q * QW, QW), QW)
        inv = mass[0:1, lanes]
        out_ref[0:24, lanes] = (r1[q, b, loc] + dir2[q, 1] + rrl2[q, 0] + res[q, 0:24]) * inv
        out_ref[24:48, lanes] = (r1[q, b, hic] + dir2[q, 0] + rrl2[q, 1] + res[q, 24:48]) * inv
        return carry

    lax.fori_loop(0, QN, close2, 0)

    def sent_q(q, carry):
        for copy in first(q) + second(q) + third(q) + fourth(q):
            copy.wait_send()
        return carry

    lax.fori_loop(0, QN, sent_q, 0)
    for k in range(1, SIDE):
        mass_copy(mx.at[0], mx, 0, k).wait_send()
        mass_copy(my.at[0], my, 1, k).wait_send()

    def sent_z(i, carry):
        to_sibling(i, own).wait_send()

        @pl.when(i > 0)
        def _():
            give_stats(i, 0).wait_send()
            give_stats(i, 1).wait_send()
            hand_out(i).wait_send()

            @pl.when(i < Z - 1)
            def _():
                hop(i, i, own, right).wait_send()
        return carry

    lax.fori_loop(0, Z, sent_z, 0)
    give_stats(0, 1 - core).wait_send()
    hop_half(13, half_a, 15, right).wait_send()
    hop_half(14, half_b, 16, left).wait_send()


def on_device(embeddings, candidates, centroids):
    f32, bf16 = jnp.float32, jnp.bfloat16
    dma = pltpu.SemaphoreType.DMA
    turned = pl.pallas_call(
        kernel,
        out_shape=jax.ShapeDtypeStruct((COLS, OWN), f32),
        in_specs=[pl.BlockSpec(memory_space=pl.ANY)] * 3,
        out_specs=pl.BlockSpec(memory_space=pltpu.VMEM),
        scratch_shapes=[
            pltpu.VMEM((Z, CHUNK, D), bf16),
            pltpu.VMEM((D, ROWS), bf16),
            pltpu.VMEM((OWN, D), bf16),
            pltpu.VMEM((ROWS, NCAND), jnp.int32),
            pltpu.VMEM((NCAND, ROWS), jnp.int32),
            pltpu.VMEM((OWN, CHUNK), f32),
            pltpu.VMEM((OWN, ROWS), f32),
            pltpu.VMEM((QW, ROWS), bf16),
            pltpu.VMEM((Z, 2, CHUNK), f32),
            pltpu.VMEM((2 * Z, 2, CHUNK), f32),
            pltpu.VMEM((Z, 2, CHUNK), f32),
            pltpu.VMEM((1, ROWS), f32),
            pltpu.VMEM((OWN, 128), f32),
            pltpu.VMEM((1, OWN), f32),
            pltpu.VMEM((SIDE, 1, OWN), f32),
            pltpu.VMEM((SIDE, 1, OWN), f32),
            pltpu.VMEM((QN, SIDE, SIDE, COLS, QW), f32),
            pltpu.VMEM((QN, 2, 2, COLS, QW), f32),
            pltpu.VMEM((QN, 2, 2, COLS, QW), f32),
            pltpu.VMEM((QN, 2, 2, COLS, QW), f32),
            pltpu.VMEM((QN, 2, 2, COLS, QW), f32),
            pltpu.VMEM((QN, SIDE, COLS, QW), f32),
            pltpu.VMEM((QN, 2, COLS // 2, QW), f32),
            pltpu.VMEM((QN, 2, COLS // 2, QW), f32),
            pltpu.VMEM((QN, 2, COLS // 2, QW), f32),
            pltpu.VMEM((QN, 2, COLS // 2, QW), f32),
            pltpu.VMEM((QN, COLS, QW), f32),
            dma((3,)),
            dma((Z + 1,)), dma((Z + 1,)),
            dma((Z,)), dma((Z,)),
            dma((2 * Z,)), dma((2 * Z,)),
            dma((Z,)), dma((Z,)),
            dma((2 * SIDE,)), dma((2 * SIDE,)),
            dma((QN * 12,)), dma((QN * 12,)),
        ],
        compiler_params=pltpu.CompilerParams(
            collective_id=0, has_side_effects=True, vmem_limit_bytes=56 * 1024 * 1024),
    )(embeddings, candidates, centroids)
    return jnp.transpose(turned)


def solution(mesh):
    placed = (P(("dp", "cent"), None), P("dp", None), P("cent", None))
    return jax.shard_map(
        on_device, mesh=mesh, in_specs=placed, out_specs=P("cent", "dp"), check_vma=False
    )
```

```python
import math

import jax
import jax.numpy as jnp
from jax import lax
from jax.experimental import pallas as pl
from jax.experimental.pallas import tpu as pltpu
from jax.sharding import PartitionSpec as P

D = 768
BLOCK = 128
Z = 16
SIDE = 4
SHARD = 64
CHUNK = 128
ROWS = Z * CHUNK
OWN = 1024
NBLK = OWN // BLOCK
COLS = 48
QN = 4
QW = OWN // QN
NCAND = 32
LOW = -1e30
FLOOR = -1e29
MESH = pl.DeviceIdType.MESH
NT = (((1,), (1,)), ((), ()))
PIECE = 16
PIECES = SHARD // PIECE
NEAR = (1, -1, 2, -2)
STRIDE = (1, -1, 2, 0)
TOP = 32766.0
TINY = 1e-30


def rem(a, b):
    return lax.rem(a, b)


def kernel(emb_hbm, cand_hbm, cent_hbm, out_ref,
           e_all, et, cent, candt, hs, x_buf, w_buf, top_buf, tot_buf, st, sb, s2, s2r, fr, fac,
           mp, mass, mx, my, s_buf, s_q, rel1, dir1, rrl1, tmp1, sc1, sc1r, st1, st1r,
           r1, r_q, rel2, dir2, rrl2, tmp2, sc2, sc2r, st2, st2r, res,
           in_sem, ag_send, ag_recv, sib_send, sib_recv, st_send, st_recv, s2_send, s2_recv,
           m_send, m_recv, rs_send, rs_recv):
    f32 = jnp.float32
    dp = lax.axis_index("dp")
    ce = lax.axis_index("cent")
    z = ce // 2
    core = rem(ce, 2)
    px = dp // SIDE
    py = rem(dp, SIDE)
    right = rem(z + 1, Z)
    left = rem(z + Z - 1, Z)
    own = pl.ds(pl.multiple_of(core * SHARD, SHARD), SHARD)

    load_e = pltpu.make_async_copy(emb_hbm, e_all.at[0, own], in_sem.at[0])
    load_c = pltpu.make_async_copy(cent_hbm, cent, in_sem.at[1])
    load_k = pltpu.make_async_copy(cand_hbm, candt, in_sem.at[2])
    load_e.start()
    load_c.start()
    load_k.start()

    barrier = pltpu.get_barrier_semaphore()

    def greet(d, c):
        pl.semaphore_signal(barrier, inc=1, device_id=(d, c), device_id_type=MESH)

    for c in range(2):
        for away in NEAR:
            greet(dp, rem(z + away + Z, Z) * 2 + c)
    greet(dp, z * 2 + 1 - core)
    for k in range(1, SIDE):
        greet(rem(px + k, SIDE) * SIDE + py, ce)
        greet(px * SIDE + rem(py + k, SIDE), ce)
    pl.semaphore_wait(barrier, 2 * len(NEAR) + 1 + 2 * (SIDE - 1))

    def hop(src, dst, p, to_z):
        rows = pl.ds(pl.multiple_of(core * SHARD + p * PIECE, PIECE), PIECE)
        return pltpu.make_async_remote_copy(
            src_ref=e_all.at[src, rows], dst_ref=e_all.at[dst, rows],
            send_sem=ag_send.at[dst * PIECES + p], recv_sem=ag_recv.at[dst * PIECES + p],
            device_id=(dp, to_z * 2 + core), device_id_type=MESH)

    def to_sibling(slot, rows):
        return pltpu.make_async_remote_copy(
            src_ref=e_all.at[slot, rows], dst_ref=e_all.at[slot, rows],
            send_sem=sib_send.at[slot], recv_sem=sib_recv.at[slot],
            device_id=(dp, z * 2 + 1 - core), device_id_type=MESH)

    other = pl.ds(pl.multiple_of((1 - core) * SHARD, SHARD), SHARD)

    load_e.wait()
    for p in range(PIECES):
        hop(0, 1, p, right).start()
        hop(0, 2, p, left).start()
    to_sibling(0, own).start()

    load_k.wait()
    load_c.wait()

    def square(b, carry):
        at = pl.ds(pl.multiple_of(b * BLOCK, BLOCK), BLOCK)
        c32 = cent[at, :].astype(f32)
        half = 0.5 * jnp.sum(c32 * c32, axis=1, keepdims=True)
        hs[at, :] = jnp.broadcast_to(half, (BLOCK, CHUNK))
        return carry

    lax.fori_loop(0, NBLK, square, 0)

    def source(i):
        odd = rem(i, 2)
        return rem(z + (1 - 2 * odd) * ((i + 1) // 2) + Z, Z)

    def give_stats(i, j):
        zs = source(i)
        return pltpu.make_async_remote_copy(
            src_ref=st.at[zs], dst_ref=sb.at[j - 1, zs],
            send_sem=st_send.at[(j - 1) * Z + zs], recv_sem=st_recv.at[(j - 1) * Z + zs],
            device_id=(dp, rem(z + 4 * j, Z) * 2 + core), device_id_type=MESH)

    scale = 1.0 / math.sqrt(D)

    def listed(i):
        return candt[:, pl.ds(pl.multiple_of(source(i) * CHUNK, CHUNK), CHUNK)]

    def logits(b, e, blocks, lanes, top):
        width = e.shape[0]
        at = slice(b * BLOCK, (b + 1) * BLOCK)
        dots = lax.dot_general(cent[at, :], e, NT, preferred_element_type=f32)
        hit = jnp.max(jnp.where(blocks == ce * NBLK + b, 1.0, 0.0), axis=0, keepdims=True)
        h = hs[at, :]
        if width > CHUNK:
            h = jnp.concatenate([h, h], axis=1)
        l = jnp.where(hit > 0.5, (dots - h) * scale, LOW)
        x_buf[at, lanes] = l
        return jnp.maximum(top, jnp.max(l.reshape(BLOCK // 8, 8, width), axis=0))

    def powers(b, m, lanes, total):
        at = slice(b * BLOCK, (b + 1) * BLOCK)
        ex = jnp.exp(x_buf[at, lanes] - m)
        x_buf[at, lanes] = ex
        return total + jnp.sum(ex.reshape(BLOCK // 8, 8, m.shape[1]), axis=0)

    def single(i):
        to_sibling(i, other).wait_recv()
        lanes = pl.ds(pl.multiple_of(i * CHUNK, CHUNK), CHUNK)
        e = e_all[i]
        blocks = listed(i)
        top = jnp.full((8, CHUNK), FLOOR, f32)
        for b in range(NBLK):
            top = logits(b, e, blocks, lanes, top)
        m = jnp.max(top, axis=0, keepdims=True)
        total = jnp.zeros((8, CHUNK), f32)
        for b in range(NBLK):
            total = powers(b, m, lanes, total)
        zs = source(i)
        st[zs, 0:1] = m
        st[zs, 1:2] = jnp.sum(total, axis=0, keepdims=True)

    def pair(u, part):
        ia, ib = 2 * u - 1, 2 * u
        lanes = pl.ds(pl.multiple_of(ia * CHUNK, CHUNK), 2 * CHUNK)
        half = NBLK // 2
        if part == 0:
            to_sibling(ia, other).wait_recv()
            to_sibling(ib, other).wait_recv()
        if part < 2:
            e = e_all[pl.ds(ia, 2)].reshape(2 * CHUNK, D)
            blocks = jnp.concatenate([listed(ia), listed(ib)], axis=1)
            top = jnp.full((8, 2 * CHUNK), FLOOR, f32) if part == 0 else top_buf[...]
            for b in range(part * half, (part + 1) * half):
                top = logits(b, e, blocks, lanes, top)
            if part == 1:
                top = jnp.broadcast_to(jnp.max(top, axis=0, keepdims=True), top.shape)
            top_buf[...] = top
        else:
            m = top_buf[0:1, :]
            total = jnp.zeros((8, 2 * CHUNK), f32) if part == 2 else tot_buf[...]
            for b in range((part - 2) * half, (part - 1) * half):
                total = powers(b, m, lanes, total)
            i = ia if part == 2 else ib
            et[:, pl.ds(pl.multiple_of(i * CHUNK, CHUNK), CHUNK)] = jnp.transpose(e_all[i])
            if part == 2:
                tot_buf[...] = total
            else:
                t = jnp.sum(total, axis=0, keepdims=True)
                za, zb = source(ia), source(ib)
                st[za, 0:1] = m[:, :CHUNK]
                st[za, 1:2] = t[:, :CHUNK]
                st[zb, 0:1] = m[:, CHUNK:]
                st[zb, 1:2] = t[:, CHUNK:]

    HALF = PIECES // 2

    def step(s, carry):
        for p in range(PIECES):
            @pl.when(s <= 7)
            def _():
                hop(2 * s - 1, 2 * s - 1, p, right).wait_recv()

                @pl.when((s <= 6) | (p < HALF))
                def _():
                    hop(2 * s - 1, 2 * s + 1, p, right).start()

                hop(2 * s, 2 * s, p, left).wait_recv()

                @pl.when(s <= 6)
                def _():
                    hop(2 * s, 2 * s + 2, p, left).start()

                if p >= HALF:
                    @pl.when(s == 7)
                    def _():
                        hop(14, 15, p, left).start()

                if p == PIECES - 1:
                    to_sibling(2 * s - 1, own).start()
                    to_sibling(2 * s, own).start()

            if p == PIECES - 1:
                @pl.when(s == 8)
                def _():
                    for k in range(PIECES):
                        hop(15, 15, k, right).wait_recv()
                    to_sibling(15, own).start()

            @pl.when((s >= 2) & (s <= 8))
            def _():
                pair(s - 1, p)

        @pl.when((s == 1) | (s == 9))
        def _():
            i = jnp.where(s == 1, 0, Z - 1)
            single(i)
            et[:, pl.ds(pl.multiple_of(i * CHUNK, CHUNK), CHUNK)] = jnp.transpose(e_all[i])

        def tell(i, c):
            give_stats(i, 1).start()
            give_stats(i, 3).start()
            return c

        def tell_far(i, c):
            give_stats(i, 2).start()
            return c

        @pl.when(s >= 4)
        def _():
            lax.fori_loop(jnp.where(s == 4, 0, 2 * s - 3), jnp.minimum(2 * s - 1, Z), tell, 0)

        @pl.when(s >= 8)
        def _():
            lax.fori_loop(jnp.where(s == 8, 0, 15), jnp.minimum(2 * s - 1, Z), tell_far, 0)

        return carry

    lax.fori_loop(1, 10, step, 0)

    def take_stats(k, carry):
        for j in range(1, SIDE):
            give_stats(k, j).wait_recv()
        return carry

    lax.fori_loop(0, Z, take_stats, 0)

    def merge(parts):
        big = parts[0][0]
        for m, _ in parts[1:]:
            big = jnp.maximum(big, m)
        tot = None
        for m, t in parts:
            term = t * jnp.exp(m - big)
            tot = term if tot is None else tot + term
        return big, tot

    big, tot = merge([(st[:, 0, :], st[:, 1, :])] + [(sb[j, :, 0, :], sb[j, :, 1, :]) for j in range(SIDE - 1)])
    s2[:, 0, :] = big
    s2[:, 1, :] = tot

    def share(k, c):
        return pltpu.make_async_remote_copy(
            src_ref=s2, dst_ref=s2r.at[2 * k + core],
            send_sem=s2_send.at[2 * k + c], recv_sem=s2_recv.at[2 * k + core],
            device_id=(dp, rem(z + STRIDE[k] + Z, Z) * 2 + c), device_id_type=MESH)

    def take_share(k, c):
        return pltpu.make_async_remote_copy(
            src_ref=s2, dst_ref=s2r.at[2 * k + c],
            send_sem=s2_send.at[2 * k + c], recv_sem=s2_recv.at[2 * k + c],
            device_id=(dp, z * 2 + 1 - core), device_id_type=MESH)

    for k in range(3):
        share(k, 0).start()
        share(k, 1).start()
    share(3, 1 - core).start()
    for k in range(3):
        take_share(k, 0).wait_recv()
        take_share(k, 1).wait_recv()
    take_share(3, 1 - core).wait_recv()
    big, tot = merge(
        [(s2[:, 0, :], s2[:, 1, :]), (s2r[6 + 1 - core, :, 0, :], s2r[6 + 1 - core, :, 1, :])]
        + [(s2r[k, :, 0, :], s2r[k, :, 1, :]) for k in range(6)])
    fr[:, 0, :] = jnp.exp(st[:, 0, :] - big) / tot

    def factor(i, carry):
        fac[0:1, pl.ds(pl.multiple_of(i * CHUNK, CHUNK), CHUNK)] = fr[source(i)]
        return carry

    lax.fori_loop(0, Z, factor, 0)

    def neighbour(q, stage, way):
        along_x = rem(q + stage + 1, 2)
        along_y = 1 - along_x
        nx = rem(px + way * along_x + SIDE, SIDE)
        ny = rem(py + way * along_y + SIDE, SIDE)
        return (nx * SIDE + ny, ce)

    def place(q, stage):
        along_x = rem(q + stage + 1, 2)
        return px * along_x + py * (1 - along_x)

    def rs(src, dst, q, stage, part, way):
        k = ((q * 2 + stage) * 5 + part) * 2 + way
        return pltpu.make_async_remote_copy(
            src_ref=src, dst_ref=dst, send_sem=rs_send.at[k], recv_sem=rs_recv.at[k],
            device_id=neighbour(q, stage, 1 - 2 * way), device_id_type=MESH)

    la, lb = slice(0, 128), slice(128, 256)
    da, db = pl.ds(0, 128), pl.ds(128, 128)

    def shift(a, k):
        return rem(a + k, SIDE)

    def opening(q, stage):
        a = place(q, stage)
        x, rel, dr, sc, scr = (s_q, rel1, dir1, sc1, sc1r) if stage == 0 else (r_q, rel2, dir2, sc2, sc2r)
        mid = (slice(None), slice(None)) if stage == 0 else (slice(None),)

        def piece(k, lanes):
            return x.at[(q, shift(a, k)) + mid + (lanes,)]
        return [
            rs(sc.at[q], scr.at[q, 0], q, stage, 3, 0),
            rs(sc.at[q], scr.at[q, 1], q, stage, 3, 1),
            rs(piece(2, da), rel.at[q, 0], q, stage, 0, 0),
            rs(piece(2, db), rel.at[q, 1], q, stage, 0, 1),
            rs(piece(1, db), dr.at[q, 0], q, stage, 1, 0),
            rs(piece(3, da), dr.at[q, 1], q, stage, 1, 1),
        ]

    def closing(q, stage):
        tmp, rrl, sc, scr = (tmp1, rrl1, st1, st1r) if stage == 0 else (tmp2, rrl2, st2, st2r)
        return [
            rs(sc.at[q, 0], scr.at[q, 0], q, stage, 4, 0),
            rs(sc.at[q, 1], scr.at[q, 1], q, stage, 4, 1),
            rs(tmp.at[q, 0], rrl.at[q, 0], q, stage, 2, 0),
            rs(tmp.at[q, 1], rrl.at[q, 1], q, stage, 2, 1),
        ]

    def peak(v, high):
        return jnp.maximum(high, jnp.max(jnp.abs(v).reshape(COLS // 8, 8, v.shape[1]), axis=0))

    def unit(high):
        return jnp.maximum(jnp.max(high, axis=0, keepdims=True) * (1.0 / TOP), TINY)

    def code(v, inv):
        return jnp.round(v * inv).astype(jnp.int32).astype(jnp.int16)

    def value(c, sc):
        return c.astype(jnp.int32).astype(f32) * sc

    SUB = 32

    def add_up(q):
        def weigh(r, c):
            at = pl.ds(pl.multiple_of(q * QW + r * SUB, SUB), SUB)
            w = x_buf[at, :] * fac[0:1, :]
            w_buf[pl.ds(pl.multiple_of(r * SUB, SUB), SUB), :] = w.astype(jnp.bfloat16)
            part = w[:, 0:128]
            for k in range(1, ROWS // 128):
                part = part + w[:, k * 128:(k + 1) * 128]
            mp[at, :] = part
            return c

        lax.fori_loop(0, QW // SUB, weigh, 0)
        swap = rem(q, 2)

        def tall(g, c):
            rows = pl.ds(pl.multiple_of(g * 384, 128), 384)
            y = lax.dot_general(et[rows, :], w_buf[...], NT, preferred_element_type=f32)
            for j in range(8):
                jx = g * 2 + j // 4
                jy = j % 4
                i0 = jx + swap * (jy - jx)
                i1 = jy + swap * (jx - jy)
                s_buf[q, i0, i1] = y[j * COLS:(j + 1) * COLS, :]
            return c

        lax.fori_loop(0, 2, tall, 0)
        a = place(q, 0)
        high = jnp.zeros((8, QW), f32)
        for k in range(1, SIDE):
            for j in range(SIDE):
                high = peak(s_buf[q, shift(a, k), j], high)
        sc = unit(high)
        sc1[q] = sc
        inv = 1.0 / sc
        for k in range(1, SIDE):
            for j in range(SIDE):
                s_q[q, shift(a, k), j] = code(s_buf[q, shift(a, k), j], inv)
        for copy in opening(q, 0):
            copy.start()

    def relay1(q):
        a = place(q, 0)
        for copy in opening(q, 0)[0:4]:
            copy.wait_recv()
        for way, lanes in ((0, la), (1, lb)):
            other_a = shift(a, 1 + 2 * way)
            sc = sc1r[q, way][:, lanes]
            high = jnp.zeros((8, 128), f32)
            for j in range(SIDE):
                v = value(rel1[q, way, j], sc) + s_buf[q, other_a, j][:, lanes]
                s_buf[q, other_a, j, :, lanes] = v
                high = peak(v, high)
            sc = unit(high)
            st1[q, way] = sc
            inv = 1.0 / sc
            for j in range(SIDE):
                tmp1[q, way, j] = code(s_buf[q, other_a, j][:, lanes], inv)
        for copy in closing(q, 0):
            copy.start()

    def close1(q):
        a = place(q, 0)
        b = place(q, 1)
        for copy in opening(q, 0)[4:6] + closing(q, 0):
            copy.wait_recv()
        high = jnp.zeros((8, QW), f32)
        for j in range(SIDE):
            j = shift(b, j)
            mine = s_buf[q, a, j]
            va = mine[:, la] + value(dir1[q, 1, j], sc1r[q, 1][:, la]) + value(rrl1[q, 0, j], st1r[q, 0])
            vb = mine[:, lb] + value(dir1[q, 0, j], sc1r[q, 0][:, lb]) + value(rrl1[q, 1, j], st1r[q, 1])
            v = jnp.concatenate([va, vb], axis=1)
            r1[q, j] = v
            high = peak(v, high)
        sc = unit(high)
        sc2[q] = sc
        inv = 1.0 / sc
        for k in range(1, SIDE):
            r_q[q, shift(b, k)] = code(r1[q, shift(b, k)], inv)
        for copy in opening(q, 1):
            copy.start()

    def relay2(q):
        b = place(q, 1)
        for copy in opening(q, 1)[0:4]:
            copy.wait_recv()
        for way, lanes in ((0, la), (1, lb)):
            v = value(rel2[q, way], sc2r[q, way][:, lanes]) + r1[q, shift(b, 1 + 2 * way)][:, lanes]
            sc = unit(peak(v, jnp.zeros((8, 128), f32)))
            st2[q, way] = sc
            tmp2[q, way] = code(v, 1.0 / sc)
        for copy in closing(q, 1):
            copy.start()

    def close2(q):
        b = place(q, 1)
        for copy in opening(q, 1)[4:6] + closing(q, 1):
            copy.wait_recv()
        mine = r1[q, b] + res[q]
        va = mine[:, la] + value(dir2[q, 1], sc2r[q, 1][:, la]) + value(rrl2[q, 0], st2r[q, 0])
        vb = mine[:, lb] + value(dir2[q, 0], sc2r[q, 0][:, lb]) + value(rrl2[q, 1], st2r[q, 1])
        lanes = pl.ds(pl.multiple_of(q * QW, QW), QW)
        out_ref[:, lanes] = jnp.concatenate([va, vb], axis=1) * mass[0:1, lanes]

    def mass_copy(src, dst, stage, k):
        along_x = 1 - stage
        nx = rem(px + k * along_x, SIDE)
        ny = rem(py + k * stage, SIDE)
        return pltpu.make_async_remote_copy(
            src_ref=src, dst_ref=dst.at[k], send_sem=m_send.at[stage * SIDE + k], recv_sem=m_recv.at[stage * SIDE + k],
            device_id=(nx * SIDE + ny, ce), device_id_type=MESH)

    def count():
        for k in range(NBLK):
            turned = jnp.transpose(mp[k * 128:(k + 1) * 128, :])
            mx[0, 0:1, k * 128:(k + 1) * 128] = jnp.sum(turned, axis=0, keepdims=True)
        for k in range(1, SIDE):
            mass_copy(mx.at[0], mx, 0, k).start()

    def count_x():
        for k in range(1, SIDE):
            mass_copy(mx.at[0], mx, 0, k).wait_recv()
        my[0] = (mx[0] + mx[1]) + (mx[2] + mx[3])
        for k in range(1, SIDE):
            mass_copy(my.at[0], my, 1, k).start()

    def count_y():
        for k in range(1, SIDE):
            mass_copy(my.at[0], my, 1, k).wait_recv()
        mass[...] = 1.0 / ((my[0] + my[1]) + (my[2] + my[3]) + 1.0)

    def old():
        pick_r = lax.broadcasted_iota(jnp.int32, (COLS, D), 0)
        pick_c = lax.broadcasted_iota(jnp.int32, (COLS, D), 1)
        pick = jnp.where(pick_c == pick_r + dp * COLS, 1.0, 0.0).astype(jnp.bfloat16)
        for b in range(QN):
            res[b] = lax.dot_general(pick, cent[b * QW:(b + 1) * QW, :], NT, preferred_element_type=f32)

    def turn(t, carry):
        @pl.when(t < QN)
        def _():
            add_up(t)

        @pl.when(t == QN - 1)
        def _():
            count()

        @pl.when((t >= 2) & (t < QN + 2))
        def _():
            relay1(t - 2)

        @pl.when(t == QN)
        def _():
            count_x()
            old()

        @pl.when((t >= 3) & (t < QN + 3))
        def _():
            close1(t - 3)

        @pl.when((t >= 4) & (t < QN + 4))
        def _():
            relay2(t - 4)

        @pl.when(t == 5)
        def _():
            count_y()

        @pl.when(t >= 5)
        def _():
            close2(t - 5)

        return carry

    lax.fori_loop(0, QN + 5, turn, 0)

    def sent_q(q, carry):
        for copy in opening(q, 0) + closing(q, 0) + opening(q, 1) + closing(q, 1):
            copy.wait_send()
        return carry

    lax.fori_loop(0, QN, sent_q, 0)
    for k in range(1, SIDE):
        mass_copy(mx.at[0], mx, 0, k).wait_send()
        mass_copy(my.at[0], my, 1, k).wait_send()

    def sent_z(i, carry):
        to_sibling(i, own).wait_send()
        for j in range(1, SIDE):
            give_stats(i, j).wait_send()

        @pl.when(i > 0)
        def _():
            for p in range(PIECES):
                hop(i, i, p, right).wait_send()
        return carry

    lax.fori_loop(0, Z, sent_z, 0)
    for k in range(3):
        share(k, 0).wait_send()
        share(k, 1).wait_send()
    share(3, 1 - core).wait_send()


def on_device(embeddings, candidates, centroids):
    f32, bf16, i16 = jnp.float32, jnp.bfloat16, jnp.int16
    dma = pltpu.SemaphoreType.DMA
    turned = pl.pallas_call(
        kernel,
        out_shape=jax.ShapeDtypeStruct((COLS, OWN), f32),
        in_specs=[pl.BlockSpec(memory_space=pl.ANY)] * 3,
        out_specs=pl.BlockSpec(memory_space=pltpu.VMEM),
        scratch_shapes=[
            pltpu.VMEM((Z, CHUNK, D), bf16),
            pltpu.VMEM((D, ROWS), bf16),
            pltpu.VMEM((OWN, D), bf16),
            pltpu.VMEM((NCAND, ROWS), jnp.int32),
            pltpu.VMEM((OWN, CHUNK), f32),
            pltpu.VMEM((OWN, ROWS), f32),
            pltpu.VMEM((QW, ROWS), bf16),
            pltpu.VMEM((8, 2 * CHUNK), f32),
            pltpu.VMEM((8, 2 * CHUNK), f32),
            pltpu.VMEM((Z, 2, CHUNK), f32),
            pltpu.VMEM((SIDE - 1, Z, 2, CHUNK), f32),
            pltpu.VMEM((Z, 2, CHUNK), f32),
            pltpu.VMEM((8, Z, 2, CHUNK), f32),
            pltpu.VMEM((Z, 1, CHUNK), f32),
            pltpu.VMEM((1, ROWS), f32),
            pltpu.VMEM((OWN, 128), f32),
            pltpu.VMEM((1, OWN), f32),
            pltpu.VMEM((SIDE, 1, OWN), f32),
            pltpu.VMEM((SIDE, 1, OWN), f32),
            pltpu.VMEM((QN, SIDE, SIDE, COLS, QW), f32),
            pltpu.VMEM((QN, SIDE, SIDE, COLS, QW), i16),
            pltpu.VMEM((QN, 2, SIDE, COLS, 128), i16),
            pltpu.VMEM((QN, 2, SIDE, COLS, 128), i16),
            pltpu.VMEM((QN, 2, SIDE, COLS, 128), i16),
            pltpu.VMEM((QN, 2, SIDE, COLS, 128), i16),
            pltpu.VMEM((QN, 1, QW), f32),
            pltpu.VMEM((QN, 2, 1, QW), f32),
            pltpu.VMEM((QN, 2, 1, 128), f32),
            pltpu.VMEM((QN, 2, 1, 128), f32),
            pltpu.VMEM((QN, SIDE, COLS, QW), f32),
            pltpu.VMEM((QN, SIDE, COLS, QW), i16),
            pltpu.VMEM((QN, 2, COLS, 128), i16),
            pltpu.VMEM((QN, 2, COLS, 128), i16),
            pltpu.VMEM((QN, 2, COLS, 128), i16),
            pltpu.VMEM((QN, 2, COLS, 128), i16),
            pltpu.VMEM((QN, 1, QW), f32),
            pltpu.VMEM((QN, 2, 1, QW), f32),
            pltpu.VMEM((QN, 2, 1, 128), f32),
            pltpu.VMEM((QN, 2, 1, 128), f32),
            pltpu.VMEM((QN, COLS, QW), f32),
            dma((3,)),
            dma((Z * PIECES,)), dma((Z * PIECES,)),
            dma((Z,)), dma((Z,)),
            dma(((SIDE - 1) * Z,)), dma(((SIDE - 1) * Z,)),
            dma((8,)), dma((8,)),
            dma((2 * SIDE,)), dma((2 * SIDE,)),
            dma((QN * 20,)), dma((QN * 20,)),
        ],
        compiler_params=pltpu.CompilerParams(
            collective_id=0, has_side_effects=True, vmem_limit_bytes=56 * 1024 * 1024),
    )(embeddings, jnp.transpose(candidates), centroids)
    return jnp.transpose(turned)


def solution(mesh):
    placed = (P(("dp", "cent"), None), P("dp", None), P("cent", None))
    return jax.shard_map(
        on_device, mesh=mesh, in_specs=placed, out_specs=P("cent", "dp"), check_vma=False
    )
```

```python
import math

import jax
import jax.numpy as jnp
from jax import lax
from jax.experimental import pallas as pl
from jax.experimental.pallas import tpu as pltpu
from jax.sharding import PartitionSpec as P

D = 768
BLOCK = 128
Z = 16
SIDE = 4
SHARD = 64
CHUNK = 128
ROWS = Z * CHUNK
OWN = 1024
NBLK = OWN // BLOCK
COLS = 48
QN = 4
QW = OWN // QN
NCAND = 32
LOW = -1e30
FLOOR = -1e29
MESH = pl.DeviceIdType.MESH
NT = (((1,), (1,)), ((), ()))
PIECE = 16
PIECES = CHUNK // PIECE
HALF = PIECES // 2
HROWS = OWN // 2
NEAR = (1, -1, 2, -2)
STRIDE = (1, -1, 2, 0)
TOP = 32766.0
TINY = 1e-30


def rem(a, b):
    return lax.rem(a, b)


def kernel(emb_hbm, cand_hbm, cent_hbm, out_ref,
           e_all, et, cent, candt, hs, x_buf, w_buf, top_buf, tot_buf, st, sb, s2, s2r, fr, fac,
           mp, mass, mx, my, s_buf, s_q, rel1, dir1, rrl1, tmp1, sc1, sc1r, st1, st1r,
           r1, r_q, rel2, sc2, sc2r, res,
           in_sem, ag_send, ag_recv, la_send, la_recv, sib_send, sib_recv, st_send, st_recv, s2_send, s2_recv,
           m_send, m_recv, rs_send, rs_recv, ac_send, ac_recv):
    f32 = jnp.float32
    dp = lax.axis_index("dp")
    ce = lax.axis_index("cent")
    z = ce // 2
    core = rem(ce, 2)
    px = dp // SIDE
    py = rem(dp, SIDE)
    ahead = rem(z + 1 - 2 * core + Z, Z)
    own = pl.ds(pl.multiple_of(core * SHARD, SHARD), SHARD)

    load_e = pltpu.make_async_copy(emb_hbm, e_all.at[0, own], in_sem.at[0])
    load_c = pltpu.make_async_copy(cent_hbm, cent, in_sem.at[1])
    load_k = pltpu.make_async_copy(cand_hbm, candt, in_sem.at[2])
    load_e.start()
    load_c.start()
    load_k.start()

    barrier = pltpu.get_barrier_semaphore()

    def greet(d, c):
        pl.semaphore_signal(barrier, inc=1, device_id=(d, c), device_id_type=MESH)

    for c in range(2):
        for away in NEAR:
            greet(dp, rem(z + away + Z, Z) * 2 + c)
    greet(dp, z * 2 + 1 - core)
    for k in range(1, SIDE):
        greet(rem(px + k, SIDE) * SIDE + py, ce)
        greet(px * SIDE + rem(py + k, SIDE), ce)
    pl.semaphore_wait(barrier, 2 * len(NEAR) + 1 + 2 * (SIDE - 1))

    def rows_of(n):
        return pl.ds(pl.multiple_of(rem(n + HALF * core, PIECES) * PIECE, PIECE), PIECE)

    def hop(src, dst, n):
        return pltpu.make_async_remote_copy(
            src_ref=e_all.at[src, rows_of(n)], dst_ref=e_all.at[dst, rows_of(n)],
            send_sem=ag_send.at[dst * PIECES + n], recv_sem=ag_recv.at[dst * PIECES + n],
            device_id=(dp, ahead * 2 + core), device_id_type=MESH)

    def last(src, n):
        return pltpu.make_async_remote_copy(
            src_ref=e_all.at[src, rows_of(n)], dst_ref=e_all.at[Z - 1, rows_of(n)],
            send_sem=la_send.at[n], recv_sem=la_recv.at[n],
            device_id=(dp, ahead * 2 + 1 - core), device_id_type=MESH)

    other = pl.ds(pl.multiple_of((1 - core) * SHARD, SHARD), SHARD)

    def to_sibling(slot, half):
        rows = other if half else own
        return pltpu.make_async_remote_copy(
            src_ref=e_all.at[slot, rows], dst_ref=e_all.at[slot, rows],
            send_sem=sib_send.at[slot * 2 + half], recv_sem=sib_recv.at[slot * 2 + half],
            device_id=(dp, z * 2 + 1 - core), device_id_type=MESH)

    load_e.wait()
    to_sibling(0, 0).start()
    for n in range(HALF):
        hop(0, 1 + core, n).start()
    to_sibling(0, 0).wait_recv()
    for n in range(HALF, PIECES):
        hop(0, 1 + core, n).start()

    load_k.wait()
    load_c.wait()

    def square(b, carry):
        at = pl.ds(pl.multiple_of(b * BLOCK, BLOCK), BLOCK)
        c32 = cent[at, :].astype(f32)
        half = 0.5 * jnp.sum(c32 * c32, axis=1, keepdims=True)
        hs[at, :] = jnp.broadcast_to(half, (BLOCK, CHUNK))
        return carry

    lax.fori_loop(0, NBLK, square, 0)

    def source(i):
        odd = rem(i, 2)
        return rem(z + (1 - 2 * odd) * ((i + 1) // 2) + Z, Z)

    def give_stats(i, k, c):
        zs = source(i)
        return pltpu.make_async_remote_copy(
            src_ref=st.at[zs], dst_ref=sb.at[2 * k + core, zs],
            send_sem=st_send.at[2 * k + c], recv_sem=st_recv.at[2 * k + core],
            device_id=(dp, rem(z + STRIDE[k] + Z, Z) * 2 + c), device_id_type=MESH)

    def all_stats(k, c):
        return pltpu.make_async_remote_copy(
            src_ref=st, dst_ref=sb.at[2 * k + c], send_sem=st_send.at[2 * k + c], recv_sem=st_recv.at[2 * k + c],
            device_id=(dp, z * 2 + 1 - core), device_id_type=MESH)

    def tell(i):
        for k in range(3):
            give_stats(i, k, 0).start()
            give_stats(i, k, 1).start()
        give_stats(i, 3, 1 - core).start()

    scale = 1.0 / math.sqrt(D)

    def listed(i):
        return candt[:, pl.ds(pl.multiple_of(source(i) * CHUNK, CHUNK), CHUNK)]

    def logits(g, e, blocks, lanes, top):
        width = e.shape[0]
        dots = lax.dot_general(cent[g * HROWS:(g + 1) * HROWS, :], e, NT, preferred_element_type=f32)
        for k in range(HROWS // BLOCK):
            b = g * (HROWS // BLOCK) + k
            at = slice(b * BLOCK, (b + 1) * BLOCK)
            hit = jnp.max(jnp.where(blocks == ce * NBLK + b, 1.0, 0.0), axis=0, keepdims=True)
            h = hs[at, :]
            if width > CHUNK:
                h = jnp.concatenate([h, h], axis=1)
            l = jnp.where(hit > 0.5, (dots[k * BLOCK:(k + 1) * BLOCK, :] - h) * scale, LOW)
            x_buf[at, lanes] = l
            top = jnp.maximum(top, jnp.max(l.reshape(BLOCK // 8, 8, width), axis=0))
        return top

    def powers(g, m, lanes, total):
        width = m.shape[1]
        for k in range(HROWS // BLOCK):
            b = g * (HROWS // BLOCK) + k
            at = slice(b * BLOCK, (b + 1) * BLOCK)
            ex = jnp.exp(x_buf[at, lanes] - m)
            x_buf[at, lanes] = ex
            total = total + jnp.sum(ex.reshape(BLOCK // 8, 8, width), axis=0)
        return total

    def record(i, m, total):
        t = jnp.sum(total, axis=0, keepdims=True)
        for k in range(m.shape[1] // CHUNK):
            zs = source(i + k)
            st[zs, 0:1] = m[:, k * CHUNK:(k + 1) * CHUNK]
            st[zs, 1:2] = t[:, k * CHUNK:(k + 1) * CHUNK]
            tell(i + k)

    def turn_over(i):
        et[:, pl.ds(pl.multiple_of(i * CHUNK, CHUNK), CHUNK)] = jnp.transpose(e_all[i])

    def single(i):
        lanes = pl.ds(pl.multiple_of(i * CHUNK, CHUNK), CHUNK)
        e = e_all[i]
        top = jnp.full((8, CHUNK), FLOOR, f32)
        for g in range(2):
            top = logits(g, e, listed(i), lanes, top)
        m = jnp.max(top, axis=0, keepdims=True)
        total = jnp.zeros((8, CHUNK), f32)
        for g in range(2):
            total = powers(g, m, lanes, total)
        record(i, m, total)
        turn_over(i)

    def pair(u, part):
        i = 2 * u - 1
        lanes = pl.ds(pl.multiple_of(i * CHUNK, CHUNK), 2 * CHUNK)
        if part == 0:
            to_sibling(2 * u - core, 0).wait_recv()
            to_sibling(2 * u - core, 1).wait_recv()
        if part < 2:
            e = e_all[pl.ds(i, 2)].reshape(2 * CHUNK, D)
            blocks = jnp.concatenate([listed(i), listed(i + 1)], axis=1)
            top = jnp.full((8, 2 * CHUNK), FLOOR, f32) if part == 0 else top_buf[...]
            top = logits(part, e, blocks, lanes, top)
            if part == 1:
                top = jnp.broadcast_to(jnp.max(top, axis=0, keepdims=True), top.shape)
            top_buf[...] = top
        else:
            m = top_buf[0:1, :]
            total = jnp.zeros((8, 2 * CHUNK), f32) if part == 2 else tot_buf[...]
            total = powers(part - 2, m, lanes, total)
            turn_over(i + part - 2)
            if part == 2:
                tot_buf[...] = total
            else:
                record(i, m, total)

    def step(s, carry):
        slot = 2 * s - 1 + core
        for n in range(PIECES):
            @pl.when(s <= 7)
            def _():
                hop(slot, slot, n).wait_recv()
                if n < HALF:
                    hop(slot, jnp.minimum(slot + 2, Z - 1), n).start()

                    @pl.when(s == 7)
                    def _():
                        last(slot, n).start()
                else:
                    @pl.when(s <= 6)
                    def _():
                        hop(slot, slot + 2, n).start()

                if n == HALF - 1:
                    to_sibling(slot, 0).start()
                if n == PIECES - 1:
                    to_sibling(slot, 1).start()

            if n % 2 == 1:
                @pl.when((s >= 2) & (s <= 8))
                def _():
                    pair(s - 1, n // 2)

        @pl.when(s == 8)
        def _():
            for n in range(HALF):
                hop(Z - 1, Z - 1, n).wait_recv()
                last(Z - 1, n).wait_recv()

        @pl.when((s == 1) | (s == 8))
        def _():
            single(jnp.where(s == 1, 0, Z - 1))

        return carry

    lax.fori_loop(1, 9, step, 0)

    def merge(parts):
        big = parts[0][0]
        for m, _ in parts[1:]:
            big = jnp.maximum(big, m)
        tot = None
        for m, t in parts:
            term = t * jnp.exp(m - big)
            tot = term if tot is None else tot + term
        return big, tot

    def both(ref, *at):
        return ref[at + (slice(None), 0)], ref[at + (slice(None), 1)]

    for k in range(3):
        all_stats(k, 0).wait_recv()
        all_stats(k, 1).wait_recv()
    all_stats(3, 1 - core).wait_recv()
    big, tot = merge([both(st), both(sb, 6 + 1 - core)] + [both(sb, k) for k in range(6)])
    s2[:, 0, :] = big
    s2[:, 1, :] = tot

    def share(j):
        return pltpu.make_async_remote_copy(
            src_ref=s2, dst_ref=s2r.at[j - 1], send_sem=s2_send.at[j - 1], recv_sem=s2_recv.at[j - 1],
            device_id=(dp, rem(z + 4 * j, Z) * 2 + core), device_id_type=MESH)

    for j in (2, 1, 3):
        share(j).start()

    pick_r = lax.broadcasted_iota(jnp.int32, (COLS, D), 0)
    pick_c = lax.broadcasted_iota(jnp.int32, (COLS, D), 1)
    pick = jnp.where(pick_c == pick_r + dp * COLS, 1.0, 0.0).astype(jnp.bfloat16)
    for b in range(QN):
        res[b] = lax.dot_general(pick, cent[b * QW:(b + 1) * QW, :], NT, preferred_element_type=f32)

    def sent_z(s, carry):
        slot = 2 * s - 1 + core
        to_sibling(slot, 0).wait_send()
        to_sibling(slot, 1).wait_send()
        for n in range(PIECES):
            hop(slot, slot, n).wait_send()
        return carry

    lax.fori_loop(1, 8, sent_z, 0)
    to_sibling(0, 0).wait_send()
    for n in range(HALF):
        hop(Z - 1, Z - 1, n).wait_send()
        last(Z - 1, n).wait_send()
    for k in range(3):
        all_stats(k, 0).wait_send()
        all_stats(k, 1).wait_send()
    all_stats(3, 1 - core).wait_send()

    for j in (1, 3, 2):
        share(j).wait_recv()
    big, tot = merge([(big, tot)] + [both(s2r, j) for j in range(SIDE - 1)])
    fr[:, 0, :] = jnp.exp(st[:, 0, :] - big) / tot

    def factor(i, carry):
        fac[0:1, pl.ds(pl.multiple_of(i * CHUNK, CHUNK), CHUNK)] = fr[source(i)]
        return carry

    lax.fori_loop(0, Z, factor, 0)

    def neighbour(q, stage, way):
        along_x = rem(q + stage + 1, 2)
        along_y = 1 - along_x
        nx = rem(px + way * along_x + SIDE, SIDE)
        ny = rem(py + way * along_y + SIDE, SIDE)
        return (nx * SIDE + ny, ce)

    def place(q, stage):
        along_x = rem(q + stage + 1, 2)
        return px * along_x + py * (1 - along_x)

    def rs(src, dst, q, part, way):
        k = (q * 5 + part) * 2 + way
        return pltpu.make_async_remote_copy(
            src_ref=src, dst_ref=dst, send_sem=rs_send.at[k], recv_sem=rs_recv.at[k],
            device_id=neighbour(q, 0, 1 - 2 * way), device_id_type=MESH)

    la, lb = slice(0, 128), slice(128, 256)
    da, db = pl.ds(0, 128), pl.ds(128, 128)

    def shift(a, k):
        return rem(a + k, SIDE)

    def opening(q):
        a = place(q, 0)

        def piece(k, lanes):
            return s_q.at[q, shift(a, k), :, :, lanes]
        return [
            rs(sc1.at[q], sc1r.at[q, 0], q, 3, 0),
            rs(sc1.at[q], sc1r.at[q, 1], q, 3, 1),
            rs(piece(2, da), rel1.at[q, 0], q, 0, 0),
            rs(piece(2, db), rel1.at[q, 1], q, 0, 1),
            rs(piece(1, db), dir1.at[q, 0], q, 1, 0),
            rs(piece(3, da), dir1.at[q, 1], q, 1, 1),
        ]

    def closing(q):
        return [
            rs(st1.at[q, 0], st1r.at[q, 0], q, 4, 0),
            rs(st1.at[q, 1], st1r.at[q, 1], q, 4, 1),
            rs(tmp1.at[q, 0], rrl1.at[q, 0], q, 2, 0),
            rs(tmp1.at[q, 1], rrl1.at[q, 1], q, 2, 1),
        ]

    def across(q):
        b = place(q, 1)
        copies = []
        for k in (2, 1, 3):
            for n, (src, dst) in enumerate(((sc2.at[q], sc2r.at[q, k]), (r_q.at[q, shift(b, k)], rel2.at[q, k]))):
                copies.append(pltpu.make_async_remote_copy(
                    src_ref=src, dst_ref=dst, send_sem=ac_send.at[q * 8 + n * 4 + k], recv_sem=ac_recv.at[q * 8 + n * 4 + k],
                    device_id=neighbour(q, 1, k), device_id_type=MESH))
        return copies

    def peak(v, high):
        return jnp.maximum(high, jnp.max(jnp.abs(v).reshape(COLS // 8, 8, v.shape[1]), axis=0))

    def unit(high):
        return jnp.maximum(jnp.max(high, axis=0, keepdims=True) * (1.0 / TOP), TINY)

    def code(v, inv):
        return jnp.round(v * inv).astype(jnp.int32).astype(jnp.int16)

    def value(c, sc):
        return c.astype(jnp.int32).astype(f32) * sc

    SUB = 32

    def add_up(q):
        def weigh(r, c):
            at = pl.ds(pl.multiple_of(q * QW + r * SUB, SUB), SUB)
            w = x_buf[at, :] * fac[0:1, :]
            w_buf[pl.ds(pl.multiple_of(r * SUB, SUB), SUB), :] = w.astype(jnp.bfloat16)
            part = w[:, 0:128]
            for k in range(1, ROWS // 128):
                part = part + w[:, k * 128:(k + 1) * 128]
            mp[at, :] = part
            return c

        lax.fori_loop(0, QW // SUB, weigh, 0)
        swap = rem(q, 2)

        y = lax.dot_general(et[...], w_buf[...], NT, preferred_element_type=f32)
        for jx in range(SIDE):
            for jy in range(SIDE):
                i0 = jx + swap * (jy - jx)
                i1 = jy + swap * (jx - jy)
                j = (jx * SIDE + jy) * COLS
                s_buf[q, i0, i1] = y[j:j + COLS, :]
        a = place(q, 0)
        high = jnp.zeros((8, QW), f32)
        for k in range(1, SIDE):
            for j in range(SIDE):
                high = peak(s_buf[q, shift(a, k), j], high)
        sc = unit(high)
        sc1[q] = sc
        inv = 1.0 / sc
        for k in range(1, SIDE):
            for j in range(SIDE):
                s_q[q, shift(a, k), j] = code(s_buf[q, shift(a, k), j], inv)

    def relay1(q):
        a = place(q, 0)
        for copy in opening(q)[0:4]:
            copy.wait_recv()
        for way, lanes in ((0, la), (1, lb)):
            other_a = shift(a, 1 + 2 * way)
            sc = sc1r[q, way][:, lanes]
            high = jnp.zeros((8, 128), f32)
            for j in range(SIDE):
                v = value(rel1[q, way, j], sc) + s_buf[q, other_a, j][:, lanes]
                s_buf[q, other_a, j, :, lanes] = v
                high = peak(v, high)
            sc = unit(high)
            st1[q, way] = sc
            inv = 1.0 / sc
            for j in range(SIDE):
                tmp1[q, way, j] = code(s_buf[q, other_a, j][:, lanes], inv)
        for copy in closing(q):
            copy.start()

    def close1(q):
        a = place(q, 0)
        b = place(q, 1)
        for copy in opening(q)[4:6] + closing(q):
            copy.wait_recv()
        high = jnp.zeros((8, QW), f32)
        for j in range(SIDE):
            j = shift(b, j)
            mine = s_buf[q, a, j]
            va = mine[:, la] + value(dir1[q, 1, j], sc1r[q, 1][:, la]) + value(rrl1[q, 0, j], st1r[q, 0])
            vb = mine[:, lb] + value(dir1[q, 0, j], sc1r[q, 0][:, lb]) + value(rrl1[q, 1, j], st1r[q, 1])
            v = jnp.concatenate([va, vb], axis=1)
            r1[q, j] = v
            high = peak(v, high)
        sc = unit(high)
        sc2[q] = sc
        inv = 1.0 / sc
        for k in range(1, SIDE):
            r_q[q, shift(b, k)] = code(r1[q, shift(b, k)], inv)
        for copy in across(q):
            copy.start()

    def close2(q):
        b = place(q, 1)
        for copy in across(q):
            copy.wait_recv()
        total = r1[q, b] + res[q]
        for k in range(1, SIDE):
            total = total + value(rel2[q, k], sc2r[q, k])
        lanes = pl.ds(pl.multiple_of(q * QW, QW), QW)
        out_ref[:, lanes] = total * mass[0:1, lanes]

    def mass_copy(src, dst, stage, k):
        along_x = 1 - stage
        nx = rem(px + k * along_x, SIDE)
        ny = rem(py + k * stage, SIDE)
        return pltpu.make_async_remote_copy(
            src_ref=src, dst_ref=dst.at[k], send_sem=m_send.at[stage * SIDE + k], recv_sem=m_recv.at[stage * SIDE + k],
            device_id=(nx * SIDE + ny, ce), device_id_type=MESH)

    def count():
        for k in range(NBLK):
            turned = jnp.transpose(mp[k * 128:(k + 1) * 128, :])
            mx[0, 0:1, k * 128:(k + 1) * 128] = jnp.sum(turned, axis=0, keepdims=True)
        for k in range(1, SIDE):
            mass_copy(mx.at[0], mx, 0, k).start()

    def count_x():
        for k in range(1, SIDE):
            mass_copy(mx.at[0], mx, 0, k).wait_recv()
        my[0] = (mx[0] + mx[1]) + (mx[2] + mx[3])
        for k in range(1, SIDE):
            mass_copy(my.at[0], my, 1, k).start()

    def count_y():
        for k in range(1, SIDE):
            mass_copy(my.at[0], my, 1, k).wait_recv()
        mass[...] = 1.0 / ((my[0] + my[1]) + (my[2] + my[3]) + 1.0)

    def turn(t, carry):
        @pl.when(t < QN)
        def _():
            add_up(t)

        @pl.when((t >= 2) & (t < QN + 2))
        def _():
            relay1(t - 2)

        @pl.when(t < QN)
        def _():
            for copy in opening(t):
                copy.start()

        @pl.when(t == QN - 1)
        def _():
            count()

        @pl.when((t >= 3) & (t < QN + 3))
        def _():
            close1(t - 3)

        @pl.when(t == 5)
        def _():
            count_x()

        @pl.when(t == 6)
        def _():
            count_y()

        @pl.when(t >= 6)
        def _():
            close2(t - 6)

        return carry

    lax.fori_loop(0, QN + 6, turn, 0)

    def sent_q(q, carry):
        for copy in opening(q) + closing(q) + across(q):
            copy.wait_send()
        return carry

    lax.fori_loop(0, QN, sent_q, 0)
    for k in range(1, SIDE):
        mass_copy(mx.at[0], mx, 0, k).wait_send()
        mass_copy(my.at[0], my, 1, k).wait_send()
        share(k).wait_send()


def on_device(embeddings, candidates, centroids):
    f32, bf16, i16 = jnp.float32, jnp.bfloat16, jnp.int16
    dma = pltpu.SemaphoreType.DMA
    turned = pl.pallas_call(
        kernel,
        out_shape=pltpu.VMEM((COLS, OWN), f32),
        in_specs=[pl.BlockSpec(memory_space=pl.ANY)] * 3,
        out_specs=pl.BlockSpec(memory_space=pltpu.VMEM),
        scratch_shapes=[
            pltpu.VMEM((Z, CHUNK, D), bf16),
            pltpu.VMEM((D, ROWS), bf16),
            pltpu.VMEM((OWN, D), bf16),
            pltpu.VMEM((NCAND, ROWS), jnp.int32),
            pltpu.VMEM((OWN, CHUNK), f32),
            pltpu.VMEM((OWN, ROWS), f32),
            pltpu.VMEM((QW, ROWS), bf16),
            pltpu.VMEM((8, 2 * CHUNK), f32),
            pltpu.VMEM((8, 2 * CHUNK), f32),
            pltpu.VMEM((Z, 2, CHUNK), f32),
            pltpu.VMEM((8, Z, 2, CHUNK), f32),
            pltpu.VMEM((Z, 2, CHUNK), f32),
            pltpu.VMEM((SIDE - 1, Z, 2, CHUNK), f32),
            pltpu.VMEM((Z, 1, CHUNK), f32),
            pltpu.VMEM((1, ROWS), f32),
            pltpu.VMEM((OWN, 128), f32),
            pltpu.VMEM((1, OWN), f32),
            pltpu.VMEM((SIDE, 1, OWN), f32),
            pltpu.VMEM((SIDE, 1, OWN), f32),
            pltpu.VMEM((QN, SIDE, SIDE, COLS, QW), f32),
            pltpu.VMEM((QN, SIDE, SIDE, COLS, QW), i16),
            pltpu.VMEM((QN, 2, SIDE, COLS, 128), i16),
            pltpu.VMEM((QN, 2, SIDE, COLS, 128), i16),
            pltpu.VMEM((QN, 2, SIDE, COLS, 128), i16),
            pltpu.VMEM((QN, 2, SIDE, COLS, 128), i16),
            pltpu.VMEM((QN, 1, QW), f32),
            pltpu.VMEM((QN, 2, 1, QW), f32),
            pltpu.VMEM((QN, 2, 1, 128), f32),
            pltpu.VMEM((QN, 2, 1, 128), f32),
            pltpu.VMEM((QN, SIDE, COLS, QW), f32),
            pltpu.VMEM((QN, SIDE, COLS, QW), i16),
            pltpu.VMEM((QN, SIDE, COLS, QW), i16),
            pltpu.VMEM((QN, 1, QW), f32),
            pltpu.VMEM((QN, SIDE, 1, QW), f32),
            pltpu.VMEM((QN, COLS, QW), f32),
            dma((3,)),
            dma((Z * PIECES,)), dma((Z * PIECES,)),
            dma((HALF,)), dma((HALF,)),
            dma((2 * Z,)), dma((2 * Z,)),
            dma((8,)), dma((8,)),
            dma((SIDE,)), dma((SIDE,)),
            dma((2 * SIDE,)), dma((2 * SIDE,)),
            dma((QN * 10,)), dma((QN * 10,)),
            dma((QN * 8,)), dma((QN * 8,)),
        ],
        compiler_params=pltpu.CompilerParams(
            collective_id=0, has_side_effects=True, vmem_limit_bytes=56 * 1024 * 1024),
    )(embeddings, jnp.transpose(candidates), centroids)
    return jnp.transpose(turned)


def solution(mesh):
    placed = (P(("dp", "cent"), None), P("dp", None), P("cent", None))
    return jax.shard_map(
        on_device, mesh=mesh, in_specs=placed, out_specs=P("cent", "dp"), check_vma=False
    )
```

```python
import math

import jax
import jax.numpy as jnp
from jax import lax
from jax.experimental import pallas as pl
from jax.experimental.pallas import tpu as pltpu
from jax.sharding import PartitionSpec as P

D = 768
BLOCK = 128
Z = 16
SIDE = 4
SHARD = 64
CHUNK = 128
ROWS = Z * CHUNK
OWN = 1024
NBLK = OWN // BLOCK
COLS = 48
QN = 4
QW = OWN // QN
NCAND = 32
LOW = -1e30
FLOOR = -1e29
MESH = pl.DeviceIdType.MESH
NT = (((1,), (1,)), ((), ()))
PIECE = 16
PIECES = CHUNK // PIECE
HALF = PIECES // 2
HROWS = OWN // 2
NEAR = (1, -1, 2, -2)
STRIDE = (1, -1, 2, 0)
TOP = 32766.0
TINY = 1e-30


def rem(a, b):
    return lax.rem(a, b)


def kernel(emb_hbm, cand_hbm, cent_hbm, out_ref,
           e_all, et, cent, candt, hs, x_buf, w_buf, top_buf, tot_buf, st, last_st, dbuf, sb, s2, s2r, fr, fac,
           mp, mass, mx, my, s_buf, s_q, rel1, dir1, rrl1, tmp1, sc1, sc1r, st1, st1r,
           r1, r_q, rel2, sc2, sc2r, res,
           in_sem, ag_send, ag_recv, la_send, la_recv, sib_send, sib_recv, st_send, st_recv, s2_send, s2_recv, db_send, db_recv,
           m_send, m_recv, rs_send, rs_recv, ac_send, ac_recv):
    f32 = jnp.float32
    dp = lax.axis_index("dp")
    ce = lax.axis_index("cent")
    z = ce // 2
    core = rem(ce, 2)
    px = dp // SIDE
    py = rem(dp, SIDE)
    facing = rem(z + Z // 2, Z)
    ahead = rem(z + 1 - 2 * core + Z, Z)
    own = pl.ds(pl.multiple_of(core * SHARD, SHARD), SHARD)

    barrier = pltpu.get_barrier_semaphore()

    def greet(d, c):
        pl.semaphore_signal(barrier, inc=1, device_id=(d, c), device_id_type=MESH)

    for c in range(2):
        for away in NEAR:
            greet(dp, rem(z + away + Z, Z) * 2 + c)
    greet(dp, z * 2 + 1 - core)
    for k in range(1, SIDE):
        greet(rem(px + k, SIDE) * SIDE + py, ce)
        greet(px * SIDE + rem(py + k, SIDE), ce)
    load_e = pltpu.make_async_copy(emb_hbm, e_all.at[0, own], in_sem.at[0])
    load_c = pltpu.make_async_copy(cent_hbm, cent, in_sem.at[1])
    load_k = pltpu.make_async_copy(cand_hbm, candt, in_sem.at[2])
    load_e.start()
    load_c.start()
    load_k.start()

    pl.semaphore_wait(barrier, 2 * len(NEAR) + 1 + 2 * (SIDE - 1))

    def rows_of(n):
        return pl.ds(pl.multiple_of(rem(n + HALF * core, PIECES) * PIECE, PIECE), PIECE)

    def hop(src, dst, n):
        return pltpu.make_async_remote_copy(
            src_ref=e_all.at[src, rows_of(n)], dst_ref=e_all.at[dst, rows_of(n)],
            send_sem=ag_send.at[dst * PIECES + n], recv_sem=ag_recv.at[dst * PIECES + n],
            device_id=(dp, ahead * 2 + core), device_id_type=MESH)

    def last(src, n):
        return pltpu.make_async_remote_copy(
            src_ref=e_all.at[src, rows_of(n)], dst_ref=e_all.at[Z - 1, rows_of(n)],
            send_sem=la_send.at[n], recv_sem=la_recv.at[n],
            device_id=(dp, ahead * 2 + 1 - core), device_id_type=MESH)

    other = pl.ds(pl.multiple_of((1 - core) * SHARD, SHARD), SHARD)

    def to_sibling(slot, half):
        rows = other if half else own
        return pltpu.make_async_remote_copy(
            src_ref=e_all.at[slot, rows], dst_ref=e_all.at[slot, rows],
            send_sem=sib_send.at[slot * 2 + half], recv_sem=sib_recv.at[slot * 2 + half],
            device_id=(dp, z * 2 + 1 - core), device_id_type=MESH)

    load_e.wait()
    to_sibling(0, 0).start()
    for n in range(HALF):
        hop(0, 1 + core, n).start()
    to_sibling(0, 0).wait_recv()
    for n in range(HALF, PIECES):
        hop(0, 1 + core, n).start()

    load_k.wait()
    load_c.wait()

    def square(b, carry):
        at = pl.ds(pl.multiple_of(b * BLOCK, BLOCK), BLOCK)
        c32 = cent[at, :].astype(f32)
        half = 0.5 * jnp.sum(c32 * c32, axis=1, keepdims=True)
        hs[at, :] = jnp.broadcast_to(half, (BLOCK, CHUNK))
        return carry

    lax.fori_loop(0, NBLK, square, 0)

    def source(i):
        odd = rem(i, 2)
        return rem(z + (1 - 2 * odd) * ((i + 1) // 2) + Z, Z)

    def give_stats(i, k, c):
        zs = source(i)
        return pltpu.make_async_remote_copy(
            src_ref=st.at[zs], dst_ref=sb.at[2 * k + core, zs],
            send_sem=st_send.at[2 * k + c], recv_sem=st_recv.at[2 * k + core],
            device_id=(dp, rem(z + STRIDE[k] + Z, Z) * 2 + c), device_id_type=MESH)

    def all_stats(k, c):
        return pltpu.make_async_remote_copy(
            src_ref=st, dst_ref=sb.at[2 * k + c], send_sem=st_send.at[2 * k + c], recv_sem=st_recv.at[2 * k + c],
            device_id=(dp, z * 2 + 1 - core), device_id_type=MESH)

    def tell(i):
        for k in range(3):
            give_stats(i, k, 0).start()
            give_stats(i, k, 1).start()
        give_stats(i, 3, 1 - core).start()

    scale = 1.0 / math.sqrt(D)

    def listed(i):
        return candt[:, pl.ds(pl.multiple_of(source(i) * CHUNK, CHUNK), CHUNK)]

    def logits(g, e, blocks, lanes, top):
        width = e.shape[0]
        dots = lax.dot_general(cent[g * HROWS:(g + 1) * HROWS, :], e, NT, preferred_element_type=f32)
        for k in range(HROWS // BLOCK):
            b = g * (HROWS // BLOCK) + k
            at = slice(b * BLOCK, (b + 1) * BLOCK)
            hit = jnp.max(jnp.where(blocks == ce * NBLK + b, 1.0, 0.0), axis=0, keepdims=True)
            h = hs[at, :]
            if width > CHUNK:
                h = jnp.concatenate([h, h], axis=1)
            l = jnp.where(hit > 0.5, (dots[k * BLOCK:(k + 1) * BLOCK, :] - h) * scale, LOW)
            x_buf[at, lanes] = l
            top = jnp.maximum(top, jnp.max(l.reshape(BLOCK // 8, 8, width), axis=0))
        return top

    def powers(g, m, lanes, total):
        width = m.shape[1]
        for k in range(HROWS // BLOCK):
            b = g * (HROWS // BLOCK) + k
            at = slice(b * BLOCK, (b + 1) * BLOCK)
            ex = jnp.exp(x_buf[at, lanes] - m)
            x_buf[at, lanes] = ex
            total = total + jnp.sum(ex.reshape(BLOCK // 8, 8, width), axis=0)
        return total

    def record(i, m, total):
        t = jnp.sum(total, axis=0, keepdims=True)
        for k in range(m.shape[1] // CHUNK):
            zs = source(i + k)
            st[zs, 0:1] = m[:, k * CHUNK:(k + 1) * CHUNK]
            st[zs, 1:2] = t[:, k * CHUNK:(k + 1) * CHUNK]
            tell(i + k)

    def turn_over(i):
        et[:, pl.ds(pl.multiple_of(i * CHUNK, CHUNK), CHUNK)] = jnp.transpose(e_all[i])

    def single(i):
        lanes = pl.ds(pl.multiple_of(i * CHUNK, CHUNK), CHUNK)
        e = e_all[i]
        top = jnp.full((8, CHUNK), FLOOR, f32)
        for g in range(2):
            top = logits(g, e, listed(i), lanes, top)
        m = jnp.max(top, axis=0, keepdims=True)
        total = jnp.zeros((8, CHUNK), f32)
        for g in range(2):
            total = powers(g, m, lanes, total)
        last_st[0:1] = m
        last_st[1:2] = jnp.sum(total, axis=0, keepdims=True)
        turn_over(i)

    def pair(u, part):
        i = 2 * u - 1
        lanes = pl.ds(pl.multiple_of(i * CHUNK, CHUNK), 2 * CHUNK)
        if part == 0:
            to_sibling(2 * u - core, 0).wait_recv()
            to_sibling(2 * u - core, 1).wait_recv()
        if part < 2:
            e = e_all[pl.ds(i, 2)].reshape(2 * CHUNK, D)
            blocks = jnp.concatenate([listed(i), listed(i + 1)], axis=1)
            top = jnp.full((8, 2 * CHUNK), FLOOR, f32) if part == 0 else top_buf[...]
            top = logits(part, e, blocks, lanes, top)
            if part == 1:
                top = jnp.broadcast_to(jnp.max(top, axis=0, keepdims=True), top.shape)
            top_buf[...] = top
        else:
            m = top_buf[0:1, :]
            total = jnp.zeros((8, 2 * CHUNK), f32) if part == 2 else tot_buf[...]
            total = powers(part - 2, m, lanes, total)
            turn_over(i + part - 2)
            if part == 2:
                tot_buf[...] = total
            else:
                record(i, m, total)

    def step(s, carry):
        slot = 2 * s - 1 + core
        for n in range(PIECES):
            @pl.when(s <= 7)
            def _():
                hop(slot, slot, n).wait_recv()
                if n < HALF:
                    hop(slot, jnp.minimum(slot + 2, Z - 1), n).start()

                    @pl.when(s == 7)
                    def _():
                        last(slot, n).start()
                else:
                    @pl.when(s <= 6)
                    def _():
                        hop(slot, slot + 2, n).start()

                if n == HALF - 1:
                    to_sibling(slot, 0).start()
                if n == PIECES - 1:
                    to_sibling(slot, 1).start()

            if n % 2 == 1:
                @pl.when((s >= 2) & (s <= 8))
                def _():
                    pair(s - 1, n // 2)

        @pl.when(s == 8)
        def _():
            for n in range(HALF):
                hop(Z - 1, Z - 1, n).wait_recv()
                last(Z - 1, n).wait_recv()

        @pl.when((s == 1) | (s == 8))
        def _():
            single(jnp.where(s == 1, 0, Z - 1))

        @pl.when(s == 1)
        def _():
            st[z] = last_st[...]
            tell(0)
            st[facing, 0:1] = jnp.full((1, CHUNK), FLOOR, f32)
            st[facing, 1:2] = jnp.zeros((1, CHUNK), f32)
            tell(Z - 1)

        return carry

    lax.fori_loop(1, 9, step, 0)

    def straight(dz, c):
        return pltpu.make_async_remote_copy(
            src_ref=last_st, dst_ref=dbuf.at[facing, core],
            send_sem=db_send.at[dz * 2 + c], recv_sem=db_recv.at[facing * 2 + core],
            device_id=(dp, rem(z + dz, Z) * 2 + c), device_id_type=MESH)

    def come(k, c):
        return pltpu.make_async_remote_copy(
            src_ref=last_st, dst_ref=dbuf.at[k, c], send_sem=db_send.at[k * 2 + c], recv_sem=db_recv.at[k * 2 + c],
            device_id=(dp, z * 2 + 1 - core), device_id_type=MESH)

    def send_straight(m, carry):
        dz = 8 + (1 - 2 * rem(m, 2)) * ((m + 1) // 2)
        straight(dz, 0).start()
        straight(dz, 1).start()
        return carry

    lax.fori_loop(0, Z - 1, send_straight, 0)
    straight(0, 1 - core).start()
    dbuf[facing, core] = last_st[...]

    def merge(parts):
        big = parts[0][0]
        for m, _ in parts[1:]:
            big = jnp.maximum(big, m)
        tot = None
        for m, t in parts:
            term = t * jnp.exp(m - big)
            tot = term if tot is None else tot + term
        return big, tot

    def both(ref, *at):
        return ref[at + (slice(None), 0)], ref[at + (slice(None), 1)]

    for k in range(3):
        all_stats(k, 0).wait_recv()
        all_stats(k, 1).wait_recv()
    all_stats(3, 1 - core).wait_recv()
    big, tot = merge([both(st), both(sb, 6 + 1 - core)] + [both(sb, k) for k in range(6)])
    s2[:, 0, :] = big
    s2[:, 1, :] = tot

    def share(j):
        return pltpu.make_async_remote_copy(
            src_ref=s2, dst_ref=s2r.at[j - 1], send_sem=s2_send.at[j - 1], recv_sem=s2_recv.at[j - 1],
            device_id=(dp, rem(z + 4 * j, Z) * 2 + core), device_id_type=MESH)

    for j in (2, 1, 3):
        share(j).start()

    pick_r = lax.broadcasted_iota(jnp.int32, (COLS, D), 0)
    pick_c = lax.broadcasted_iota(jnp.int32, (COLS, D), 1)
    pick = jnp.where(pick_c == pick_r + dp * COLS, 1.0, 0.0).astype(jnp.bfloat16)
    for b in range(QN):
        res[b] = lax.dot_general(pick, cent[b * QW:(b + 1) * QW, :], NT, preferred_element_type=f32)

    def sent_z(s, carry):
        slot = 2 * s - 1 + core
        to_sibling(slot, 0).wait_send()
        to_sibling(slot, 1).wait_send()
        for n in range(PIECES):
            hop(slot, slot, n).wait_send()
        return carry

    lax.fori_loop(1, 8, sent_z, 0)
    to_sibling(0, 0).wait_send()
    for n in range(HALF):
        hop(Z - 1, Z - 1, n).wait_send()
        last(Z - 1, n).wait_send()
    for k in range(3):
        all_stats(k, 0).wait_send()
        all_stats(k, 1).wait_send()
    all_stats(3, 1 - core).wait_send()

    for j in (1, 3, 2):
        share(j).wait_recv()

    def take_straight(k, carry):
        for c in range(2):
            @pl.when((k != facing) | (core != c))
            def _():
                come(k, c).wait_recv()
        return carry

    lax.fori_loop(0, Z, take_straight, 0)
    big, tot = merge(
        [(big, tot)] + [both(s2r, j) for j in range(SIDE - 1)] + [(dbuf[:, c, 0, :], dbuf[:, c, 1, :]) for c in range(2)])
    row = lax.broadcasted_iota(jnp.int32, (Z, CHUNK), 0)
    mine = jnp.where(row == facing, last_st[0:1], st[:, 0, :])
    fr[:, 0, :] = jnp.exp(mine - big) / tot

    def factor(i, carry):
        fac[0:1, pl.ds(pl.multiple_of(i * CHUNK, CHUNK), CHUNK)] = fr[source(i)]
        return carry

    lax.fori_loop(0, Z, factor, 0)

    def neighbour(q, stage, way):
        along_x = rem(q + stage + 1, 2)
        along_y = 1 - along_x
        nx = rem(px + way * along_x + SIDE, SIDE)
        ny = rem(py + way * along_y + SIDE, SIDE)
        return (nx * SIDE + ny, ce)

    def place(q, stage):
        along_x = rem(q + stage + 1, 2)
        return px * along_x + py * (1 - along_x)

    def rs(src, dst, q, part, way):
        k = (q * 5 + part) * 2 + way
        return pltpu.make_async_remote_copy(
            src_ref=src, dst_ref=dst, send_sem=rs_send.at[k], recv_sem=rs_recv.at[k],
            device_id=neighbour(q, 0, 1 - 2 * way), device_id_type=MESH)

    la, lb = slice(0, 128), slice(128, 256)
    da, db = pl.ds(0, 128), pl.ds(128, 128)

    def shift(a, k):
        return rem(a + k, SIDE)

    def opening(q):
        a = place(q, 0)

        def piece(k, lanes):
            return s_q.at[q, shift(a, k), :, :, lanes]
        return [
            rs(sc1.at[q], sc1r.at[q, 0], q, 3, 0),
            rs(sc1.at[q], sc1r.at[q, 1], q, 3, 1),
            rs(piece(2, da), rel1.at[q, 0], q, 0, 0),
            rs(piece(2, db), rel1.at[q, 1], q, 0, 1),
            rs(piece(1, db), dir1.at[q, 0], q, 1, 0),
            rs(piece(3, da), dir1.at[q, 1], q, 1, 1),
        ]

    def closing(q):
        return [
            rs(st1.at[q, 0], st1r.at[q, 0], q, 4, 0),
            rs(st1.at[q, 1], st1r.at[q, 1], q, 4, 1),
            rs(tmp1.at[q, 0], rrl1.at[q, 0], q, 2, 0),
            rs(tmp1.at[q, 1], rrl1.at[q, 1], q, 2, 1),
        ]

    def across(q):
        b = place(q, 1)
        copies = []
        for k in (2, 1, 3):
            for n, (src, dst) in enumerate(((sc2.at[q], sc2r.at[q, k]), (r_q.at[q, shift(b, k)], rel2.at[q, k]))):
                copies.append(pltpu.make_async_remote_copy(
                    src_ref=src, dst_ref=dst, send_sem=ac_send.at[q * 8 + n * 4 + k], recv_sem=ac_recv.at[q * 8 + n * 4 + k],
                    device_id=neighbour(q, 1, k), device_id_type=MESH))
        return copies

    def peak(v, high):
        return jnp.maximum(high, jnp.max(jnp.abs(v).reshape(COLS // 8, 8, v.shape[1]), axis=0))

    def unit(high):
        return jnp.maximum(jnp.max(high, axis=0, keepdims=True) * (1.0 / TOP), TINY)

    def code(v, inv):
        return jnp.round(v * inv).astype(jnp.int32).astype(jnp.int16)

    def value(c, sc):
        return c.astype(jnp.int32).astype(f32) * sc

    SUB = 32

    def add_up(q):
        for k in range(ROWS // QW):
            cols = slice(k * QW, (k + 1) * QW)
            f = fac[0:1, cols]
            for r in range(QW // SUB):
                at = pl.ds(pl.multiple_of(q * QW + r * SUB, SUB), SUB)
                w = x_buf[at, cols] * f
                w_buf[r * SUB:(r + 1) * SUB, cols] = w.astype(jnp.bfloat16)
                part = w[:, 0:128] + w[:, 128:256]
                mp[at, :] = part if k == 0 else mp[at, :] + part
        swap = rem(q, 2)

        y = lax.dot_general(et[...], w_buf[...], NT, preferred_element_type=f32)
        for jx in range(SIDE):
            for jy in range(SIDE):
                i0 = jx + swap * (jy - jx)
                i1 = jy + swap * (jx - jy)
                j = (jx * SIDE + jy) * COLS
                s_buf[q, i0, i1] = y[j:j + COLS, :]
        a = place(q, 0)
        high = jnp.zeros((8, QW), f32)
        for k in range(1, SIDE):
            for j in range(SIDE):
                high = peak(s_buf[q, shift(a, k), j], high)
        sc = unit(high)
        sc1[q] = sc
        inv = 1.0 / sc
        for k in range(1, SIDE):
            for j in range(SIDE):
                s_q[q, shift(a, k), j] = code(s_buf[q, shift(a, k), j], inv)

    def relay1(q):
        a = place(q, 0)
        for copy in opening(q)[0:4]:
            copy.wait_recv()
        for way, lanes in ((0, la), (1, lb)):
            other_a = shift(a, 1 + 2 * way)
            sc = sc1r[q, way][:, lanes]
            high = jnp.zeros((8, 128), f32)
            for j in range(SIDE):
                v = value(rel1[q, way, j], sc) + s_buf[q, other_a, j][:, lanes]
                s_buf[q, other_a, j, :, lanes] = v
                high = peak(v, high)
            sc = unit(high)
            st1[q, way] = sc
            inv = 1.0 / sc
            for j in range(SIDE):
                tmp1[q, way, j] = code(s_buf[q, other_a, j][:, lanes], inv)
        for copy in closing(q):
            copy.start()

    def close1(q):
        a = place(q, 0)
        b = place(q, 1)
        for copy in opening(q)[4:6] + closing(q):
            copy.wait_recv()
        high = jnp.zeros((8, QW), f32)
        for j in range(SIDE):
            j = shift(b, j)
            mine = s_buf[q, a, j]
            va = mine[:, la] + value(dir1[q, 1, j], sc1r[q, 1][:, la]) + value(rrl1[q, 0, j], st1r[q, 0])
            vb = mine[:, lb] + value(dir1[q, 0, j], sc1r[q, 0][:, lb]) + value(rrl1[q, 1, j], st1r[q, 1])
            v = jnp.concatenate([va, vb], axis=1)
            r1[q, j] = v
            high = peak(v, high)
        sc = unit(high)
        sc2[q] = sc
        inv = 1.0 / sc
        for k in range(1, SIDE):
            r_q[q, shift(b, k)] = code(r1[q, shift(b, k)], inv)
        for copy in across(q):
            copy.start()

    def close2(q):
        b = place(q, 1)
        for copy in across(q):
            copy.wait_recv()
        total = r1[q, b] + res[q]
        for k in range(1, SIDE):
            total = total + value(rel2[q, k], sc2r[q, k])
        lanes = pl.ds(pl.multiple_of(q * QW, QW), QW)
        out_ref[:, lanes] = total * mass[0:1, lanes]

    def mass_copy(src, dst, stage, k):
        along_x = 1 - stage
        nx = rem(px + k * along_x, SIDE)
        ny = rem(py + k * stage, SIDE)
        return pltpu.make_async_remote_copy(
            src_ref=src, dst_ref=dst.at[k], send_sem=m_send.at[stage * SIDE + k], recv_sem=m_recv.at[stage * SIDE + k],
            device_id=(nx * SIDE + ny, ce), device_id_type=MESH)

    def count():
        for k in range(NBLK):
            turned = jnp.transpose(mp[k * 128:(k + 1) * 128, :])
            mx[0, 0:1, k * 128:(k + 1) * 128] = jnp.sum(turned, axis=0, keepdims=True)
        for k in range(1, SIDE):
            mass_copy(mx.at[0], mx, 0, k).start()

    def count_x():
        for k in range(1, SIDE):
            mass_copy(mx.at[0], mx, 0, k).wait_recv()
        my[0] = (mx[0] + mx[1]) + (mx[2] + mx[3])
        for k in range(1, SIDE):
            mass_copy(my.at[0], my, 1, k).start()

    def count_y():
        for k in range(1, SIDE):
            mass_copy(my.at[0], my, 1, k).wait_recv()
        mass[...] = 1.0 / ((my[0] + my[1]) + (my[2] + my[3]) + 1.0)

    def turn(t, carry):
        @pl.when(t < QN)
        def _():
            add_up(t)

        @pl.when((t >= 3) & (t < QN + 3))
        def _():
            relay1(t - 3)

        @pl.when(t < QN)
        def _():
            for copy in opening(t):
                copy.start()

        @pl.when(t == QN - 1)
        def _():
            count()

        @pl.when((t >= 6) & (t < QN + 6))
        def _():
            close1(t - 6)

        @pl.when(t == 7)
        def _():
            count_x()

        @pl.when(t == 9)
        def _():
            count_y()

        @pl.when(t >= 9)
        def _():
            close2(t - 9)

        return carry

    lax.fori_loop(0, QN + 9, turn, 0)

    def sent_q(q, carry):
        for copy in opening(q) + closing(q) + across(q):
            copy.wait_send()
        return carry

    lax.fori_loop(0, QN, sent_q, 0)
    def sent_straight(dz, carry):
        straight(dz, 0).wait_send()
        straight(dz, 1).wait_send()
        return carry

    lax.fori_loop(1, Z, sent_straight, 0)
    straight(0, 1 - core).wait_send()
    for k in range(1, SIDE):
        mass_copy(mx.at[0], mx, 0, k).wait_send()
        mass_copy(my.at[0], my, 1, k).wait_send()
        share(k).wait_send()


def on_device(embeddings, candidates, centroids):
    f32, bf16, i16 = jnp.float32, jnp.bfloat16, jnp.int16
    dma = pltpu.SemaphoreType.DMA
    turned = pl.pallas_call(
        kernel,
        out_shape=pltpu.VMEM((COLS, OWN), f32),
        in_specs=[pl.BlockSpec(memory_space=pl.ANY)] * 3,
        out_specs=pl.BlockSpec(memory_space=pltpu.VMEM),
        scratch_shapes=[
            pltpu.VMEM((Z, CHUNK, D), bf16),
            pltpu.VMEM((D, ROWS), bf16),
            pltpu.VMEM((OWN, D), bf16),
            pltpu.VMEM((NCAND, ROWS), jnp.int32),
            pltpu.VMEM((OWN, CHUNK), f32),
            pltpu.VMEM((OWN, ROWS), f32),
            pltpu.VMEM((QW, ROWS), bf16),
            pltpu.VMEM((8, 2 * CHUNK), f32),
            pltpu.VMEM((8, 2 * CHUNK), f32),
            pltpu.VMEM((Z, 2, CHUNK), f32),
            pltpu.VMEM((2, CHUNK), f32),
            pltpu.VMEM((Z, 2, 2, CHUNK), f32),
            pltpu.VMEM((8, Z, 2, CHUNK), f32),
            pltpu.VMEM((Z, 2, CHUNK), f32),
            pltpu.VMEM((SIDE - 1, Z, 2, CHUNK), f32),
            pltpu.VMEM((Z, 1, CHUNK), f32),
            pltpu.VMEM((1, ROWS), f32),
            pltpu.VMEM((OWN, 128), f32),
            pltpu.VMEM((1, OWN), f32),
            pltpu.VMEM((SIDE, 1, OWN), f32),
            pltpu.VMEM((SIDE, 1, OWN), f32),
            pltpu.VMEM((QN, SIDE, SIDE, COLS, QW), f32),
            pltpu.VMEM((QN, SIDE, SIDE, COLS, QW), i16),
            pltpu.VMEM((QN, 2, SIDE, COLS, 128), i16),
            pltpu.VMEM((QN, 2, SIDE, COLS, 128), i16),
            pltpu.VMEM((QN, 2, SIDE, COLS, 128), i16),
            pltpu.VMEM((QN, 2, SIDE, COLS, 128), i16),
            pltpu.VMEM((QN, 1, QW), f32),
            pltpu.VMEM((QN, 2, 1, QW), f32),
            pltpu.VMEM((QN, 2, 1, 128), f32),
            pltpu.VMEM((QN, 2, 1, 128), f32),
            pltpu.VMEM((QN, SIDE, COLS, QW), f32),
            pltpu.VMEM((QN, SIDE, COLS, QW), i16),
            pltpu.VMEM((QN, SIDE, COLS, QW), i16),
            pltpu.VMEM((QN, 1, QW), f32),
            pltpu.VMEM((QN, SIDE, 1, QW), f32),
            pltpu.VMEM((QN, COLS, QW), f32),
            dma((3,)),
            dma((Z * PIECES,)), dma((Z * PIECES,)),
            dma((HALF,)), dma((HALF,)),
            dma((2 * Z,)), dma((2 * Z,)),
            dma((8,)), dma((8,)),
            dma((SIDE,)), dma((SIDE,)),
            dma((2 * Z,)), dma((2 * Z,)),
            dma((2 * SIDE,)), dma((2 * SIDE,)),
            dma((QN * 10,)), dma((QN * 10,)),
            dma((QN * 8,)), dma((QN * 8,)),
        ],
        compiler_params=pltpu.CompilerParams(
            collective_id=0, has_side_effects=True, vmem_limit_bytes=56 * 1024 * 1024),
    )(embeddings, jnp.transpose(candidates), centroids)
    return jnp.transpose(turned)


def solution(mesh):
    placed = (P(("dp", "cent"), None), P("dp", None), P("cent", None))
    return jax.shard_map(
        on_device, mesh=mesh, in_specs=placed, out_specs=P("cent", "dp"), check_vma=False
    )
```

```python
import math

import jax
import jax.numpy as jnp
from jax import lax
from jax.experimental import pallas as pl
from jax.experimental.pallas import tpu as pltpu
from jax.sharding import PartitionSpec as P

D = 768
BLOCK = 128
Z = 16
SIDE = 4
SHARD = 64
CHUNK = 128
ROWS = Z * CHUNK
OWN = 1024
NBLK = OWN // BLOCK
COLS = 48
QN = 4
QW = OWN // QN
NCAND = 32
LOW = -1e30
FLOOR = -1e29
MESH = pl.DeviceIdType.MESH
NT = (((1,), (1,)), ((), ()))
PIECE = 16
PIECES = CHUNK // PIECE
HALF = PIECES // 2
HROWS = OWN // 2
NEAR = (1, -1, 2, -2)
STRIDE = (1, -1, 2, 0)
TOP = 32766.0
TINY = 1e-30


def rem(a, b):
    return lax.rem(a, b)


def kernel(emb_hbm, cand_hbm, cent_hbm, out_ref,
           e_all, et, cent, candt, hs, x_buf, w_buf, top_buf, tot_buf, st, last_st, dbuf, sb, s2, s2r, fr, fac,
           mp, mass, mx, my, s_buf, s_q, rel1, dir1, rrl1, tmp1, sc1, sc1r, st1, st1r,
           r1, r_q, rel2, sc2, sc2r, res,
           in_sem, ag_send, ag_recv, la_send, la_recv, sib_send, sib_recv, st_send, st_recv, s2_send, s2_recv, db_send, db_recv,
           m_send, m_recv, rs_send, rs_recv, ac_send, ac_recv):
    f32 = jnp.float32
    dp = lax.axis_index("dp")
    ce = lax.axis_index("cent")
    z = ce // 2
    core = rem(ce, 2)
    px = dp // SIDE
    py = rem(dp, SIDE)
    facing = rem(z + Z // 2, Z)
    ahead = rem(z + 1 - 2 * core + Z, Z)
    own = pl.ds(pl.multiple_of(core * SHARD, SHARD), SHARD)

    barrier = pltpu.get_barrier_semaphore()

    def greet(d, c):
        pl.semaphore_signal(barrier, inc=1, device_id=(d, c), device_id_type=MESH)

    for c in range(2):
        for away in NEAR:
            greet(dp, rem(z + away + Z, Z) * 2 + c)
    greet(dp, z * 2 + 1 - core)
    for k in range(1, SIDE):
        greet(rem(px + k, SIDE) * SIDE + py, ce)
        greet(px * SIDE + rem(py + k, SIDE), ce)
    load_e = pltpu.make_async_copy(emb_hbm, e_all.at[0, own], in_sem.at[0])
    load_c = pltpu.make_async_copy(cent_hbm, cent, in_sem.at[1])
    load_k = pltpu.make_async_copy(cand_hbm, candt, in_sem.at[2])
    load_e.start()
    load_c.start()
    load_k.start()

    pl.semaphore_wait(barrier, 2 * len(NEAR) + 1 + 2 * (SIDE - 1))

    def rows_of(n):
        return pl.ds(pl.multiple_of(rem(n + HALF * core, PIECES) * PIECE, PIECE), PIECE)

    def hop(src, dst, n):
        return pltpu.make_async_remote_copy(
            src_ref=e_all.at[src, rows_of(n)], dst_ref=e_all.at[dst, rows_of(n)],
            send_sem=ag_send.at[dst * PIECES + n], recv_sem=ag_recv.at[dst * PIECES + n],
            device_id=(dp, ahead * 2 + core), device_id_type=MESH)

    def last(src, n):
        return pltpu.make_async_remote_copy(
            src_ref=e_all.at[src, rows_of(n)], dst_ref=e_all.at[Z - 1, rows_of(n)],
            send_sem=la_send.at[n], recv_sem=la_recv.at[n],
            device_id=(dp, ahead * 2 + 1 - core), device_id_type=MESH)

    other = pl.ds(pl.multiple_of((1 - core) * SHARD, SHARD), SHARD)

    def to_sibling(slot, half):
        rows = other if half else own
        return pltpu.make_async_remote_copy(
            src_ref=e_all.at[slot, rows], dst_ref=e_all.at[slot, rows],
            send_sem=sib_send.at[slot * 2 + half], recv_sem=sib_recv.at[slot * 2 + half],
            device_id=(dp, z * 2 + 1 - core), device_id_type=MESH)

    load_e.wait()
    to_sibling(0, 0).start()
    for n in range(HALF):
        hop(0, 1 + core, n).start()
    to_sibling(0, 0).wait_recv()
    for n in range(HALF, PIECES):
        hop(0, 1 + core, n).start()

    load_k.wait()
    load_c.wait()

    def square(b, carry):
        at = pl.ds(pl.multiple_of(b * BLOCK, BLOCK), BLOCK)
        c32 = cent[at, :].astype(f32)
        half = 0.5 * jnp.sum(c32 * c32, axis=1, keepdims=True)
        hs[at, :] = jnp.broadcast_to(half, (BLOCK, CHUNK))
        return carry

    lax.fori_loop(0, NBLK, square, 0)

    def source(i):
        odd = rem(i, 2)
        return rem(z + (1 - 2 * odd) * ((i + 1) // 2) + Z, Z)

    def give_stats(i, k, c):
        zs = source(i)
        return pltpu.make_async_remote_copy(
            src_ref=st.at[zs], dst_ref=sb.at[2 * k + core, zs],
            send_sem=st_send.at[2 * k + c], recv_sem=st_recv.at[2 * k + core],
            device_id=(dp, rem(z + STRIDE[k] + Z, Z) * 2 + c), device_id_type=MESH)

    def all_stats(k, c):
        return pltpu.make_async_remote_copy(
            src_ref=st, dst_ref=sb.at[2 * k + c], send_sem=st_send.at[2 * k + c], recv_sem=st_recv.at[2 * k + c],
            device_id=(dp, z * 2 + 1 - core), device_id_type=MESH)

    def tell(i):
        for k in range(3):
            give_stats(i, k, 0).start()
            give_stats(i, k, 1).start()
        give_stats(i, 3, 1 - core).start()

    scale = 1.0 / math.sqrt(D)

    def listed(i):
        return candt[:, pl.ds(pl.multiple_of(source(i) * CHUNK, CHUNK), CHUNK)]

    def logits(g, e, blocks, lanes, top):
        width = e.shape[0]
        dots = lax.dot_general(cent[g * HROWS:(g + 1) * HROWS, :], e, NT, preferred_element_type=f32)
        for k in range(HROWS // BLOCK):
            b = g * (HROWS // BLOCK) + k
            at = slice(b * BLOCK, (b + 1) * BLOCK)
            hit = jnp.max(jnp.where(blocks == ce * NBLK + b, 1.0, 0.0), axis=0, keepdims=True)
            h = hs[at, :]
            if width > CHUNK:
                h = jnp.concatenate([h, h], axis=1)
            l = jnp.where(hit > 0.5, (dots[k * BLOCK:(k + 1) * BLOCK, :] - h) * scale, LOW)
            x_buf[at, lanes] = l
            top = jnp.maximum(top, jnp.max(l.reshape(BLOCK // 8, 8, width), axis=0))
        return top

    def powers(g, m, lanes, total):
        width = m.shape[1]
        for k in range(HROWS // BLOCK):
            b = g * (HROWS // BLOCK) + k
            at = slice(b * BLOCK, (b + 1) * BLOCK)
            ex = jnp.exp(x_buf[at, lanes] - m)
            x_buf[at, lanes] = ex
            total = total + jnp.sum(ex.reshape(BLOCK // 8, 8, width), axis=0)
        return total

    def record(i, m, total):
        t = jnp.sum(total, axis=0, keepdims=True)
        for k in range(m.shape[1] // CHUNK):
            zs = source(i + k)
            st[zs, 0:1] = m[:, k * CHUNK:(k + 1) * CHUNK]
            st[zs, 1:2] = t[:, k * CHUNK:(k + 1) * CHUNK]
            tell(i + k)

    def turn_over(i):
        et[:, pl.ds(pl.multiple_of(i * CHUNK, CHUNK), CHUNK)] = jnp.transpose(e_all[i])

    def single(i):
        lanes = pl.ds(pl.multiple_of(i * CHUNK, CHUNK), CHUNK)
        e = e_all[i]
        top = jnp.full((8, CHUNK), FLOOR, f32)
        for g in range(2):
            top = logits(g, e, listed(i), lanes, top)
        m = jnp.max(top, axis=0, keepdims=True)
        total = jnp.zeros((8, CHUNK), f32)
        for g in range(2):
            total = powers(g, m, lanes, total)
        last_st[0:1] = m
        last_st[1:2] = jnp.sum(total, axis=0, keepdims=True)
        turn_over(i)

    def pair(u, part):
        i = 2 * u - 1
        lanes = pl.ds(pl.multiple_of(i * CHUNK, CHUNK), 2 * CHUNK)
        if part == 0:
            to_sibling(2 * u - core, 0).wait_recv()
            to_sibling(2 * u - core, 1).wait_recv()
        if part < 2:
            e = e_all[pl.ds(i, 2)].reshape(2 * CHUNK, D)
            blocks = jnp.concatenate([listed(i), listed(i + 1)], axis=1)
            top = jnp.full((8, 2 * CHUNK), FLOOR, f32) if part == 0 else top_buf[...]
            top = logits(part, e, blocks, lanes, top)
            if part == 1:
                top = jnp.broadcast_to(jnp.max(top, axis=0, keepdims=True), top.shape)
            top_buf[...] = top
        else:
            m = top_buf[0:1, :]
            total = jnp.zeros((8, 2 * CHUNK), f32) if part == 2 else tot_buf[...]
            total = powers(part - 2, m, lanes, total)
            turn_over(i + part - 2)
            if part == 2:
                tot_buf[...] = total
            else:
                record(i, m, total)

    def step(s, carry):
        slot = 2 * s - 1 + core
        for n in range(PIECES):
            @pl.when(s <= 7)
            def _():
                hop(slot, slot, n).wait_recv()
                if n < HALF:
                    hop(slot, jnp.minimum(slot + 2, Z - 1), n).start()

                    @pl.when(s == 7)
                    def _():
                        last(slot, n).start()
                else:
                    @pl.when(s <= 6)
                    def _():
                        hop(slot, slot + 2, n).start()

                if n == HALF - 1:
                    to_sibling(slot, 0).start()
                if n == PIECES - 1:
                    to_sibling(slot, 1).start()

            if n % 2 == 1:
                @pl.when((s >= 2) & (s <= 8))
                def _():
                    pair(s - 1, n // 2)

        @pl.when(s == 8)
        def _():
            for n in range(HALF):
                hop(Z - 1, Z - 1, n).wait_recv()
                last(Z - 1, n).wait_recv()

        @pl.when((s == 1) | (s == 8))
        def _():
            single(jnp.where(s == 1, 0, Z - 1))

        @pl.when(s == 1)
        def _():
            st[z] = last_st[...]
            tell(0)
            st[facing, 0:1] = jnp.full((1, CHUNK), FLOOR, f32)
            st[facing, 1:2] = jnp.zeros((1, CHUNK), f32)
            tell(Z - 1)

        return carry

    lax.fori_loop(1, 9, step, 0)

    def straight(dz, c):
        return pltpu.make_async_remote_copy(
            src_ref=last_st, dst_ref=dbuf.at[facing, core],
            send_sem=db_send.at[dz * 2 + c], recv_sem=db_recv.at[facing * 2 + core],
            device_id=(dp, rem(z + dz, Z) * 2 + c), device_id_type=MESH)

    def come(k, c):
        return pltpu.make_async_remote_copy(
            src_ref=last_st, dst_ref=dbuf.at[k, c], send_sem=db_send.at[k * 2 + c], recv_sem=db_recv.at[k * 2 + c],
            device_id=(dp, z * 2 + 1 - core), device_id_type=MESH)

    def send_straight(m, carry):
        dz = 8 + (1 - 2 * rem(m, 2)) * ((m + 1) // 2)
        straight(dz, 0).start()
        straight(dz, 1).start()
        return carry

    lax.fori_loop(0, Z - 1, send_straight, 0)
    straight(0, 1 - core).start()
    dbuf[facing, core] = last_st[...]

    def merge(parts):
        big = parts[0][0]
        for m, _ in parts[1:]:
            big = jnp.maximum(big, m)
        tot = None
        for m, t in parts:
            term = t * jnp.exp(m - big)
            tot = term if tot is None else tot + term
        return big, tot

    def both(ref, *at):
        return ref[at + (slice(None), 0)], ref[at + (slice(None), 1)]

    for k in range(3):
        all_stats(k, 0).wait_recv()
        all_stats(k, 1).wait_recv()
    all_stats(3, 1 - core).wait_recv()
    big, tot = merge([both(st), both(sb, 6 + 1 - core)] + [both(sb, k) for k in range(6)])
    s2[:, 0, :] = big
    s2[:, 1, :] = tot

    def share(j):
        return pltpu.make_async_remote_copy(
            src_ref=s2, dst_ref=s2r.at[j - 1], send_sem=s2_send.at[j - 1], recv_sem=s2_recv.at[j - 1],
            device_id=(dp, rem(z + 4 * j, Z) * 2 + core), device_id_type=MESH)

    for j in (2, 1, 3):
        share(j).start()

    pick_r = lax.broadcasted_iota(jnp.int32, (COLS, D), 0)
    pick_c = lax.broadcasted_iota(jnp.int32, (COLS, D), 1)
    pick = jnp.where(pick_c == pick_r + dp * COLS, 1.0, 0.0).astype(jnp.bfloat16)
    for b in range(QN):
        res[b] = lax.dot_general(pick, cent[b * QW:(b + 1) * QW, :], NT, preferred_element_type=f32)

    def sent_z(s, carry):
        slot = 2 * s - 1 + core
        to_sibling(slot, 0).wait_send()
        to_sibling(slot, 1).wait_send()
        for n in range(PIECES):
            hop(slot, slot, n).wait_send()
        return carry

    lax.fori_loop(1, 8, sent_z, 0)
    to_sibling(0, 0).wait_send()
    for n in range(HALF):
        hop(Z - 1, Z - 1, n).wait_send()
        last(Z - 1, n).wait_send()
    for k in range(3):
        all_stats(k, 0).wait_send()
        all_stats(k, 1).wait_send()
    all_stats(3, 1 - core).wait_send()

    for j in (1, 3, 2):
        share(j).wait_recv()

    def take_straight(k, carry):
        for c in range(2):
            @pl.when((k != facing) | (core != c))
            def _():
                come(k, c).wait_recv()
        return carry

    lax.fori_loop(0, Z, take_straight, 0)
    big, tot = merge(
        [(big, tot)] + [both(s2r, j) for j in range(SIDE - 1)] + [(dbuf[:, c, 0, :], dbuf[:, c, 1, :]) for c in range(2)])
    row = lax.broadcasted_iota(jnp.int32, (Z, CHUNK), 0)
    mine = jnp.where(row == facing, last_st[0:1], st[:, 0, :])
    fr[:, 0, :] = jnp.exp(mine - big) / tot

    def factor(i, carry):
        fac[0:1, pl.ds(pl.multiple_of(i * CHUNK, CHUNK), CHUNK)] = fr[source(i)]
        return carry

    lax.fori_loop(0, Z, factor, 0)

    def neighbour(q, stage, way):
        along_x = rem(q + stage + 1, 2)
        along_y = 1 - along_x
        nx = rem(px + way * along_x + SIDE, SIDE)
        ny = rem(py + way * along_y + SIDE, SIDE)
        return (nx * SIDE + ny, ce)

    def place(q, stage):
        along_x = rem(q + stage + 1, 2)
        return px * along_x + py * (1 - along_x)

    def rs(src, dst, q, part, way):
        k = (q * 5 + part) * 2 + way
        return pltpu.make_async_remote_copy(
            src_ref=src, dst_ref=dst, send_sem=rs_send.at[k], recv_sem=rs_recv.at[k],
            device_id=neighbour(q, 0, 1 - 2 * way), device_id_type=MESH)

    la, lb = slice(0, 128), slice(128, 256)
    da, db = pl.ds(0, 128), pl.ds(128, 128)

    def shift(a, k):
        return rem(a + k, SIDE)

    def opening(q):
        a = place(q, 0)

        def piece(k, lanes):
            return s_q.at[q, shift(a, k), :, :, lanes]
        return [
            rs(sc1.at[q], sc1r.at[q, 0], q, 3, 0),
            rs(sc1.at[q], sc1r.at[q, 1], q, 3, 1),
            rs(piece(2, da), rel1.at[q, 0], q, 0, 0),
            rs(piece(2, db), rel1.at[q, 1], q, 0, 1),
            rs(piece(1, db), dir1.at[q, 0], q, 1, 0),
            rs(piece(3, da), dir1.at[q, 1], q, 1, 1),
        ]

    def closing(q):
        return [
            rs(st1.at[q, 0], st1r.at[q, 0], q, 4, 0),
            rs(st1.at[q, 1], st1r.at[q, 1], q, 4, 1),
            rs(tmp1.at[q, 0], rrl1.at[q, 0], q, 2, 0),
            rs(tmp1.at[q, 1], rrl1.at[q, 1], q, 2, 1),
        ]

    def across(q):
        b = place(q, 1)
        copies = []
        for k in (2, 1, 3):
            for n, (src, dst) in enumerate(((sc2.at[q], sc2r.at[q, k]), (r_q.at[q, shift(b, k)], rel2.at[q, k]))):
                copies.append(pltpu.make_async_remote_copy(
                    src_ref=src, dst_ref=dst, send_sem=ac_send.at[q * 8 + n * 4 + k], recv_sem=ac_recv.at[q * 8 + n * 4 + k],
                    device_id=neighbour(q, 1, k), device_id_type=MESH))
        return copies

    def peak(v, high):
        return jnp.maximum(high, jnp.max(jnp.abs(v).reshape(COLS // 8, 8, v.shape[1]), axis=0))

    def unit(high):
        return jnp.maximum(jnp.max(high, axis=0, keepdims=True) * (1.0 / TOP), TINY)

    def code(v, inv):
        return jnp.round(v * inv).astype(jnp.int32).astype(jnp.int16)

    def value(c, sc):
        return c.astype(jnp.int32).astype(f32) * sc

    SUB = 32

    def add_up(q):
        for k in range(ROWS // QW):
            cols = slice(k * QW, (k + 1) * QW)
            f = fac[0:1, cols]
            for r in range(QW // SUB):
                at = pl.ds(pl.multiple_of(q * QW + r * SUB, SUB), SUB)
                w = x_buf[at, cols] * f
                w_buf[r * SUB:(r + 1) * SUB, cols] = w.astype(jnp.bfloat16)
                part = w[:, 0:128] + w[:, 128:256]
                mp[at, :] = part if k == 0 else mp[at, :] + part
        swap = rem(q, 2)

        y = lax.dot_general(et[...], w_buf[...], NT, preferred_element_type=f32)
        for jx in range(SIDE):
            for jy in range(SIDE):
                i0 = jx + swap * (jy - jx)
                i1 = jy + swap * (jx - jy)
                j = (jx * SIDE + jy) * COLS
                s_buf[q, i0, i1] = y[j:j + COLS, :]
        a = place(q, 0)
        high = jnp.zeros((8, QW), f32)
        for k in range(1, SIDE):
            for j in range(SIDE):
                high = peak(s_buf[q, shift(a, k), j], high)
        sc = unit(high)
        sc1[q] = sc
        inv = 1.0 / sc
        for k in range(1, SIDE):
            for j in range(SIDE):
                s_q[q, shift(a, k), j] = code(s_buf[q, shift(a, k), j], inv)

    def relay1(q):
        a = place(q, 0)
        for copy in opening(q)[0:4]:
            copy.wait_recv()
        for way, lanes in ((0, la), (1, lb)):
            other_a = shift(a, 1 + 2 * way)
            sc = sc1r[q, way][:, lanes]
            high = jnp.zeros((8, 128), f32)
            for j in range(SIDE):
                v = value(rel1[q, way, j], sc) + s_buf[q, other_a, j][:, lanes]
                s_buf[q, other_a, j, :, lanes] = v
                high = peak(v, high)
            sc = unit(high)
            st1[q, way] = sc
            inv = 1.0 / sc
            for j in range(SIDE):
                tmp1[q, way, j] = code(s_buf[q, other_a, j][:, lanes], inv)
        for copy in closing(q):
            copy.start()

    def close1(q):
        a = place(q, 0)
        b = place(q, 1)
        for copy in opening(q)[4:6] + closing(q):
            copy.wait_recv()
        high = jnp.zeros((8, QW), f32)
        for j in range(SIDE):
            j = shift(b, j)
            mine = s_buf[q, a, j]
            va = mine[:, la] + value(dir1[q, 1, j], sc1r[q, 1][:, la]) + value(rrl1[q, 0, j], st1r[q, 0])
            vb = mine[:, lb] + value(dir1[q, 0, j], sc1r[q, 0][:, lb]) + value(rrl1[q, 1, j], st1r[q, 1])
            v = jnp.concatenate([va, vb], axis=1)
            r1[q, j] = v
            high = peak(v, high)
        sc = unit(high)
        sc2[q] = sc
        inv = 1.0 / sc
        for k in range(1, SIDE):
            r_q[q, shift(b, k)] = code(r1[q, shift(b, k)], inv)
        for copy in across(q):
            copy.start()

    def close2(q):
        b = place(q, 1)
        for copy in across(q):
            copy.wait_recv()
        total = r1[q, b] + res[q]
        for k in range(1, SIDE):
            total = total + value(rel2[q, k], sc2r[q, k])
        lanes = pl.ds(pl.multiple_of(q * QW, QW), QW)
        out_ref[:, lanes] = total * mass[0:1, lanes]

    def mass_copy(src, dst, stage, k):
        along_x = 1 - stage
        nx = rem(px + k * along_x, SIDE)
        ny = rem(py + k * stage, SIDE)
        return pltpu.make_async_remote_copy(
            src_ref=src, dst_ref=dst.at[k], send_sem=m_send.at[stage * SIDE + k], recv_sem=m_recv.at[stage * SIDE + k],
            device_id=(nx * SIDE + ny, ce), device_id_type=MESH)

    def count():
        for k in range(NBLK):
            turned = jnp.transpose(mp[k * 128:(k + 1) * 128, :])
            mx[0, 0:1, k * 128:(k + 1) * 128] = jnp.sum(turned, axis=0, keepdims=True)
        for k in range(1, SIDE):
            mass_copy(mx.at[0], mx, 0, k).start()

    def count_x():
        for k in range(1, SIDE):
            mass_copy(mx.at[0], mx, 0, k).wait_recv()
        my[0] = (mx[0] + mx[1]) + (mx[2] + mx[3])
        for k in range(1, SIDE):
            mass_copy(my.at[0], my, 1, k).start()

    def count_y():
        for k in range(1, SIDE):
            mass_copy(my.at[0], my, 1, k).wait_recv()
        mass[...] = 1.0 / ((my[0] + my[1]) + (my[2] + my[3]) + 1.0)

    def turn(t, carry):
        @pl.when(t < QN)
        def _():
            add_up(t)

        @pl.when((t >= 3) & (t < QN + 3))
        def _():
            relay1(t - 3)

        @pl.when(t < QN)
        def _():
            for copy in opening(t)[0:4]:
                copy.start()

        @pl.when((t >= 1) & (t < QN + 1))
        def _():
            for copy in opening(t - 1)[4:6]:
                copy.start()

        @pl.when(t == QN - 1)
        def _():
            count()

        @pl.when((t >= 6) & (t < QN + 6))
        def _():
            close1(t - 6)

        @pl.when(t == 7)
        def _():
            count_x()

        @pl.when(t == 9)
        def _():
            count_y()

        @pl.when(t >= 9)
        def _():
            close2(t - 9)

        return carry

    lax.fori_loop(0, QN + 9, turn, 0)

    def sent_q(q, carry):
        for copy in opening(q) + closing(q) + across(q):
            copy.wait_send()
        return carry

    lax.fori_loop(0, QN, sent_q, 0)
    def sent_straight(dz, carry):
        straight(dz, 0).wait_send()
        straight(dz, 1).wait_send()
        return carry

    lax.fori_loop(1, Z, sent_straight, 0)
    straight(0, 1 - core).wait_send()
    for k in range(1, SIDE):
        mass_copy(mx.at[0], mx, 0, k).wait_send()
        mass_copy(my.at[0], my, 1, k).wait_send()
        share(k).wait_send()


def on_device(embeddings, candidates, centroids):
    f32, bf16, i16 = jnp.float32, jnp.bfloat16, jnp.int16
    dma = pltpu.SemaphoreType.DMA
    turned = pl.pallas_call(
        kernel,
        out_shape=pltpu.VMEM((COLS, OWN), f32),
        in_specs=[pl.BlockSpec(memory_space=pl.ANY)] * 3,
        out_specs=pl.BlockSpec(memory_space=pltpu.VMEM),
        scratch_shapes=[
            pltpu.VMEM((Z, CHUNK, D), bf16),
            pltpu.VMEM((D, ROWS), bf16),
            pltpu.VMEM((OWN, D), bf16),
            pltpu.VMEM((NCAND, ROWS), jnp.int32),
            pltpu.VMEM((OWN, CHUNK), f32),
            pltpu.VMEM((OWN, ROWS), f32),
            pltpu.VMEM((QW, ROWS), bf16),
            pltpu.VMEM((8, 2 * CHUNK), f32),
            pltpu.VMEM((8, 2 * CHUNK), f32),
            pltpu.VMEM((Z, 2, CHUNK), f32),
            pltpu.VMEM((2, CHUNK), f32),
            pltpu.VMEM((Z, 2, 2, CHUNK), f32),
            pltpu.VMEM((8, Z, 2, CHUNK), f32),
            pltpu.VMEM((Z, 2, CHUNK), f32),
            pltpu.VMEM((SIDE - 1, Z, 2, CHUNK), f32),
            pltpu.VMEM((Z, 1, CHUNK), f32),
            pltpu.VMEM((1, ROWS), f32),
            pltpu.VMEM((OWN, 128), f32),
            pltpu.VMEM((1, OWN), f32),
            pltpu.VMEM((SIDE, 1, OWN), f32),
            pltpu.VMEM((SIDE, 1, OWN), f32),
            pltpu.VMEM((QN, SIDE, SIDE, COLS, QW), f32),
            pltpu.VMEM((QN, SIDE, SIDE, COLS, QW), i16),
            pltpu.VMEM((QN, 2, SIDE, COLS, 128), i16),
            pltpu.VMEM((QN, 2, SIDE, COLS, 128), i16),
            pltpu.VMEM((QN, 2, SIDE, COLS, 128), i16),
            pltpu.VMEM((QN, 2, SIDE, COLS, 128), i16),
            pltpu.VMEM((QN, 1, QW), f32),
            pltpu.VMEM((QN, 2, 1, QW), f32),
            pltpu.VMEM((QN, 2, 1, 128), f32),
            pltpu.VMEM((QN, 2, 1, 128), f32),
            pltpu.VMEM((QN, SIDE, COLS, QW), f32),
            pltpu.VMEM((QN, SIDE, COLS, QW), i16),
            pltpu.VMEM((QN, SIDE, COLS, QW), i16),
            pltpu.VMEM((QN, 1, QW), f32),
            pltpu.VMEM((QN, SIDE, 1, QW), f32),
            pltpu.VMEM((QN, COLS, QW), f32),
            dma((3,)),
            dma((Z * PIECES,)), dma((Z * PIECES,)),
            dma((HALF,)), dma((HALF,)),
            dma((2 * Z,)), dma((2 * Z,)),
            dma((8,)), dma((8,)),
            dma((SIDE,)), dma((SIDE,)),
            dma((2 * Z,)), dma((2 * Z,)),
            dma((2 * SIDE,)), dma((2 * SIDE,)),
            dma((QN * 10,)), dma((QN * 10,)),
            dma((QN * 8,)), dma((QN * 8,)),
        ],
        compiler_params=pltpu.CompilerParams(
            collective_id=0, has_side_effects=True, vmem_limit_bytes=56 * 1024 * 1024),
    )(embeddings, jnp.transpose(candidates), centroids)
    return jnp.transpose(turned)


def solution(mesh):
    placed = (P(("dp", "cent"), None), P("dp", None), P("cent", None))
    return jax.shard_map(
        on_device, mesh=mesh, in_specs=placed, out_specs=P("cent", "dp"), check_vma=False
    )
```
